512 devices in a mesh: bins: 64 (over z, y), params: 8 (over x, core).
Axes of the slice: x: 4, y: 4, z: 16, core: 2. Of those that a mesh axis runs over, the one named last changes fastest.
Arguments:
- event_bins: int32 [196608], P('bins'), may hold values from 0 to 65535, as said below
- event_weights: bfloat16 [196608, 3072], P('bins', 'params'), may hold values from -6 to 6
- nominal: bfloat16 [196608], P('bins'), may hold values from 0.5 to 2
- background: float32 [65536], P('bins'), may hold values from 1 to 10
- observed: float32 [65536], P('bins'), may hold values from 1 to 100
Outputs:
- hessian: float32 [3072, 1920], P(('params', 'bins'))
The draws below stay inside these ranges and needn't reach their ends.
Inputs may be any that keep to these rules, and one draw needn't show every extreme that they name: `event_bins`: each index of bins holds 3072 consecutive events in ascending bin order. The owner of bin b is b // 1024; each owner's bins receive from one index of bins between 24 and 72 of its events, and in every draw every index of bins has some owner that receives exactly 72 of its events.
All inputs are finite; a program needn't handle non-finite values.
Results may differ from the reference program's by a relative error of at most 0.0016.
Values may be sent and summed in bfloat16 or wider, within the bound.
No kernel may reach another device: no remote copies, remote signals or barrier semaphores. Data moves between devices by JAX's collectives and lax.ppermute only.
A program may use at most 64 MiB of HBM per device.

```python
import math
import jax
import jax.numpy as jnp
from jax import lax

P_SIZE = 3072
BINS_DEV = 1024
E_DEV = 3072
PG = 384
NB = 65536
EVENTS = 196608
COLS = 1920
N_BINS = 64
N_PARAMS = 8


def draw_event_bins(key, part):
    base_count = E_DEV // N_BINS
    swing_most = base_count // 2

    def one_source(subkey):
        key_swing, key_perm, key_bins = jax.random.split(subkey, 3)
        swing = jax.random.randint(key_swing, (N_BINS // 2,), -swing_most, swing_most + 1)
        swing = swing.at[0].set(swing_most)
        profile = jnp.concatenate([base_count + swing, base_count - swing])
        counts = profile[jax.random.permutation(key_perm, N_BINS)]
        bounds = jnp.cumsum(counts)
        ordinal = jnp.arange(E_DEV, dtype=jnp.int32)
        target = jnp.sum((bounds[None, :] <= ordinal[:, None]).astype(jnp.int32), axis=1)
        inside = jax.random.randint(key_bins, (E_DEV,), 0, BINS_DEV)
        return jnp.sort(target * BINS_DEV + inside).astype(jnp.int32)
    source_keys = jax.random.split(jax.random.fold_in(key, 7), N_BINS)
    return jax.vmap(one_source)(source_keys).reshape(-1)


def steps_of(stream_key, shape, pieces, least, top_value):
    factor_of = 1.0
    for dim, parts in pieces:
        draws = jax.random.uniform(jax.random.fold_in(jax.random.fold_in(stream_key, 6), dim), (parts,), jnp.float32, least / len(pieces), top_value / len(pieces))
        factor_of = factor_of * jnp.repeat(jnp.exp(draws), shape[dim] // parts).reshape((-1,) + (1,) * (len(shape) - 1 - dim))
    return factor_of


def gaussian(key, extent, scale, limit, cuts=(), kind=jnp.bfloat16):
    result = scale * jax.random.normal(key, extent, jnp.float32)
    if cuts:
        result = result * steps_of(key, extent, cuts, -0.22, 0.18)
    return jnp.clip(result, -limit, limit).astype(kind)


def setup_inputs(seed: int = 0) -> dict:
    keys = jax.random.split(jax.random.key(seed), 6)
    return {
        "event_bins": draw_event_bins(jax.random.fold_in(keys[5], 71), 0),
        "event_weights": gaussian(keys[1], (EVENTS, P_SIZE), 1.0, 6.0, ((0, 64), (1, 8))),
        "nominal": jnp.clip(jnp.exp(math.log(2.0) - 1.3862944 * jax.random.uniform(keys[2], (EVENTS,), jnp.float32) ** steps_of(keys[2], (EVENTS,), ((0, 64),), -0.2, 0.2)), 0.5, 2.0).astype(jnp.bfloat16),
        "background": jnp.clip(jnp.exp(math.log(10.0) - 2.3025851 * jax.random.uniform(keys[3], (NB,), jnp.float32) ** steps_of(keys[3], (NB,), ((0, 64),), -0.2, 0.2)), 1.0, 10.0),
        "observed": jnp.clip(jnp.exp(math.log(100.0) - 4.6051702 * jax.random.uniform(keys[4], (NB,), jnp.float32) ** steps_of(keys[4], (NB,), ((0, 64),), -0.2, 0.2)), 1.0, 100.0),
    }


def reference(event_bins, event_weights, nominal, background, observed):
    bins_split = event_bins.reshape(N_BINS, E_DEV)
    weights_split = event_weights.reshape(N_BINS, E_DEV, P_SIZE)

    def add_source(carry, stacked):
        source_bins, source_weights = stacked
        part_sum = jax.ops.segment_sum(source_weights.astype(jnp.float32), source_bins, num_segments=NB)
        return carry + part_sum, None

    histogram, _ = lax.scan(add_source, jnp.zeros((NB, P_SIZE), jnp.float32), (bins_split, weights_split))
    templates = histogram.astype(jnp.bfloat16)
    nominal_sum = jax.ops.segment_sum(nominal.astype(jnp.float32), event_bins, num_segments=NB)
    yields = background + nominal_sum
    curvature = observed / (yields * yields)
    weighted = (curvature[:, None] * templates.astype(jnp.float32)).astype(jnp.bfloat16)
    dims = (((0,), (0,)), ((), ()))
    full = lax.dot_general(weighted, templates, dims, preferred_element_type=jnp.float32)
    full = full * (1.0 / NB)
    blocks = full.reshape(N_PARAMS, PG, N_PARAMS, PG)
    groups = jnp.arange(N_PARAMS, dtype=jnp.int32)
    tiles = []
    for offset in range(N_PARAMS // 2 + 1):
        tiles.append(blocks[groups, :, (groups + offset) % N_PARAMS, :])
    stacked_tiles = jnp.stack(tiles, axis=2)
    return stacked_tiles.reshape(P_SIZE, COLS)
```

```python
import functools

import jax
import jax.numpy as jnp
import numpy as np
from jax import lax
from jax.experimental import pallas as pl
from jax.experimental.pallas import tpu as pltpu
from jax.sharding import Mesh
from jax.sharding import PartitionSpec as P

BINS = ("bins_0", "bins_1")
PARAMS_BINS = ("params", "bins_0", "bins_1")
CAP = 72
EXTRA = 8
WIN = 96
COLS = 128
KB = 512
VMEM = pl.BlockSpec(memory_space=pltpu.VMEM)
SMEM = pl.BlockSpec(memory_space=pltpu.SMEM)
PARAMS = pltpu.CompilerParams(vmem_limit_bytes=40 * 2**20)


def cost(flops, moved):
    return pl.CostEstimate(flops=flops, bytes_accessed=moved, transcendentals=0)


def pick_rows(start, w_ref, events, cols):
    base = jnp.minimum((start // 16) * 16, events - WIN)
    base = pl.multiple_of(base, 16)
    off = start - base
    row = lax.broadcasted_iota(jnp.int32, (CAP, WIN), 0)
    col = lax.broadcasted_iota(jnp.int32, (CAP, WIN), 1)
    choose = jnp.where(col == row + off, 1.0, 0.0).astype(jnp.bfloat16)
    window = w_ref[pl.ds(base, WIN), cols]
    return jnp.dot(choose, window, preferred_element_type=jnp.float32)


def pack_first(owners, bins_dev, events, starts_ref, info_ref, w_ref, out_ref):
    lines = lax.broadcasted_iota(jnp.int32, (EXTRA, 128), 0)

    def one(o, _):
        start = starts_ref[o]
        rows = pick_rows(start, w_ref, events, slice(0, COLS))
        at = jnp.minimum((start // 128) * 128, events - 256)
        at = pl.multiple_of(at, 128)
        span = pltpu.roll(info_ref[:, pl.ds(at, 256)], 256 - (start - at), 1)[:, :128]
        local = span[0:1].astype(jnp.int32) - o * bins_dev
        inside = (local >= 0) & (local < bins_dev)
        high = jnp.where(inside, local // 32, -1).astype(jnp.float32)
        low = jnp.where(inside, local % 32, 0).astype(jnp.float32)
        nominal = jnp.where(inside, span[1:2], 0.0)
        extra = jnp.where(lines == 0, high, jnp.where(lines == 1, low, jnp.where(lines == 2, nominal, 0.0)))
        out_ref[o] = jnp.concatenate([rows, extra], axis=0).astype(jnp.bfloat16)
        return 0

    lax.fori_loop(0, owners, one, 0, unroll=4)


def pack_rest(owners, events, starts_ref, w_ref, *out_refs):
    def one(o, _):
        start = starts_ref[o]
        rows = pick_rows(start, w_ref, events, slice(COLS, 3 * COLS)).astype(jnp.bfloat16)
        for i, out_ref in enumerate(out_refs):
            out_ref[o] = rows[:, i * COLS : (i + 1) * COLS]
        return 0

    lax.fori_loop(0, owners, one, 0, unroll=4)


def one_hot_of(bins_ref, at, bins_dev):
    ids = lax.broadcasted_iota(jnp.int32, (bins_dev, KB), 0)
    return jnp.where(ids == bins_ref[:, pl.ds(at, KB)], 1.0, 0.0).astype(jnp.bfloat16)


def hist_first(bins_ref, nominal_ref, rows_ref, background_ref, observed_ref, out_ref, curve_ref, acc, acc_n):
    bins_dev = out_ref.shape[0]
    acc[...] = jnp.zeros_like(acc)
    acc_n[...] = jnp.zeros_like(acc_n)

    def one(i, _):
        at = pl.multiple_of(i * KB, KB)
        hot = one_hot_of(bins_ref, at, bins_dev)
        acc[...] += jnp.dot(hot, rows_ref[pl.ds(at, KB), :], preferred_element_type=jnp.float32)
        acc_n[...] += lax.dot_general(
            hot, nominal_ref[:, pl.ds(at, KB)], (((1,), (1,)), ((), ())), preferred_element_type=jnp.float32
        )
        return 0

    lax.fori_loop(0, rows_ref.shape[0] // KB, one, 0)
    out_ref[...] = acc[...].astype(jnp.bfloat16)
    yields = background_ref[...] + acc_n[:, 0:1]
    curve_ref[...] = observed_ref[...] / (yields * yields)


def hist_next(bins_ref, rows_ref, out_ref, acc):
    bins_dev = out_ref.shape[0]
    acc[...] = jnp.zeros_like(acc)

    def one(i, _):
        at = pl.multiple_of(i * KB, KB)
        hot = one_hot_of(bins_ref, at, bins_dev)
        acc[...] += jnp.dot(hot, rows_ref[pl.ds(at, KB), :], preferred_element_type=jnp.float32)
        return 0

    lax.fori_loop(0, rows_ref.shape[0] // KB, one, 0)
    out_ref[...] = acc[...].astype(jnp.bfloat16)


def gram(turns, curve_ref, order_ref, *refs):
    parts, out_ref = refs[:-1], refs[-1]
    chunks = len(parts) // turns
    own = jnp.concatenate([parts[c][...] for c in range(chunks)], axis=1)
    weighted = (curve_ref[...] * own.astype(jnp.float32)).astype(jnp.bfloat16)
    lhs = lax.dot_general(
        order_ref[...], weighted, (((1,), (1,)), ((), ())), preferred_element_type=jnp.float32
    ).astype(jnp.bfloat16)
    width = own.shape[1]
    step = out_ref.shape[1]
    for k in range(turns):
        partner = jnp.concatenate([parts[k * chunks + c][...] for c in range(chunks)], axis=1)
        full = jnp.dot(lhs, partner, preferred_element_type=jnp.float32).astype(jnp.bfloat16)
        for y in range(out_ref.shape[0]):
            out_ref[y, :, k * width : (k + 1) * width] = full[y * step : (y + 1) * step]


def from_behind(value, axis, steps):
    count = lax.axis_size(axis)
    pairs = [(source, (source + steps) % count) for source in range(count)]
    return lax.ppermute(value, axis, pairs)


def exchange(value, axis):
    return lax.all_to_all(value, axis, split_axis=0, concat_axis=0, tiled=True)


def body(event_bins, event_weights, nominal, background, observed):
    bf16, f32 = jnp.bfloat16, jnp.float32
    n0, n1 = (lax.axis_size(a) for a in BINS)
    owners = n0 * n1
    groups = lax.axis_size("params")
    events, width = event_weights.shape
    bins_dev = background.shape[0]
    chunks = width // COLS
    targets = jnp.arange(owners, dtype=jnp.int32)
    starts = jnp.sum((event_bins[None, :] < targets[:, None] * bins_dev).astype(jnp.int32), axis=1)
    info = jnp.stack([event_bins.astype(f32), nominal.astype(f32)])
    info = jnp.concatenate([info, jnp.zeros((6, events), f32)])

    slab = CAP + EXTRA
    send0 = pl.pallas_call(
        functools.partial(pack_first, owners, bins_dev, events),
        out_shape=jax.ShapeDtypeStruct((owners, slab, COLS), bf16),
        in_specs=[SMEM, VMEM, VMEM],
        out_specs=VMEM,
        compiler_params=PARAMS,
        cost_estimate=cost(2 * owners * CAP * WIN * COLS, 2 * owners * slab * COLS * 2),
        name="pack_first",
    )(starts, info, event_weights)
    rest = pl.pallas_call(
        functools.partial(pack_rest, owners, events),
        out_shape=[jax.ShapeDtypeStruct((owners, CAP, COLS), bf16)] * (chunks - 1),
        in_specs=[SMEM, VMEM],
        out_specs=[VMEM] * (chunks - 1),
        compiler_params=PARAMS,
        cost_estimate=cost(4 * owners * CAP * WIN * COLS, 4 * owners * CAP * COLS * 2),
        name="pack_rest",
    )(starts, event_weights)
    got0 = exchange(send0, BINS)
    got = [exchange(s, BINS) for s in rest]

    extra = got0[:, CAP:, :CAP].astype(f32)
    local = (extra[:, 0] * 32.0 + extra[:, 1]).astype(jnp.int32)
    local_wide = jnp.pad(local, ((0, 0), (0, EXTRA)), constant_values=-1).reshape(1, owners * slab)
    local = local.reshape(1, owners * CAP)
    nom = jnp.pad(extra[:, 2], ((0, 0), (0, EXTRA))).astype(bf16).reshape(1, owners * slab)
    nom = jnp.broadcast_to(nom, (8, owners * slab))
    tile = jax.ShapeDtypeStruct((bins_dev, COLS), bf16)
    acc = pltpu.VMEM((bins_dev, COLS), f32)
    first, curve = pl.pallas_call(
        hist_first,
        out_shape=[tile, jax.ShapeDtypeStruct((bins_dev, 1), f32)],
        in_specs=[VMEM] * 5,
        out_specs=[VMEM] * 2,
        scratch_shapes=[acc, pltpu.VMEM((bins_dev, 8), f32)],
        compiler_params=PARAMS,
        cost_estimate=cost(2 * owners * slab * bins_dev * 256, owners * slab * COLS * 2),
        name="hist_first",
    )(
        local_wide,
        nom,
        got0.reshape(owners * slab, COLS),
        background.reshape(bins_dev, 1),
        observed.reshape(bins_dev, 1),
    )
    tiles = [first]
    for g in got:
        tiles.append(
            pl.pallas_call(
                hist_next,
                out_shape=tile,
                in_specs=[VMEM] * 2,
                out_specs=VMEM,
                scratch_shapes=[acc],
                compiler_params=PARAMS,
                cost_estimate=cost(2 * owners * CAP * bins_dev * 256, owners * CAP * COLS * 2),
                name="hist_next",
            )(local, g.reshape(owners * CAP, COLS))
        )
    turns = groups // 2 + 1
    moved = [[from_behind(t, "params", -k) if k else t for t in tiles] for k in range(turns)]

    lines = width // owners
    j = np.arange(width)
    source = ((j % (width // n1)) // lines * n1 + j // (width // n1)) * lines + j % lines
    order = np.zeros((width, width), np.float32)
    order[j, source] = 1.0
    partial = pl.pallas_call(
        functools.partial(gram, turns),
        out_shape=jax.ShapeDtypeStruct((n1, width // n1, turns * width), bf16),
        in_specs=[VMEM] * (2 + turns * chunks),
        out_specs=VMEM,
        compiler_params=PARAMS,
        cost_estimate=cost(2 * bins_dev * width * width * (turns + 1), turns * width * bins_dev * 2),
        name="gram",
    )(curve, jnp.asarray(order, bf16), *[t for row in moved for t in row])
    across = exchange(partial, BINS[1]).astype(f32).sum(axis=0).astype(bf16)
    along = exchange(across.reshape(n0, lines, turns * width), BINS[0]).astype(f32).sum(axis=0)
    return along * (1.0 / (bins_dev * owners))


def solution(mesh):
    split = Mesh(mesh.devices.reshape(16, 4, mesh.shape["params"]), ("bins_0", "bins_1", "params"))
    placed = (P(BINS), P(BINS, "params"), P(BINS), P(BINS), P(BINS))
    return jax.shard_map(
        body, mesh=split, in_specs=placed, out_specs=P(PARAMS_BINS, None), check_vma=False
    )
```

```python
import functools

import jax
import jax.numpy as jnp
import numpy as np
from jax import lax
from jax.experimental import pallas as pl
from jax.experimental.pallas import tpu as pltpu
from jax.sharding import Mesh
from jax.sharding import PartitionSpec as P

BINS = ("bins_0", "bins_1")
PARAMS_BINS = ("params", "bins_0", "bins_1")
CAP = 72
EXTRA = 8
WIN = 96
COLS = 128
KB = 512
VMEM = pl.BlockSpec(memory_space=pltpu.VMEM)
SMEM = pl.BlockSpec(memory_space=pltpu.SMEM)
PARAMS = pltpu.CompilerParams(vmem_limit_bytes=40 * 2**20)


def cost(flops, moved):
    return pl.CostEstimate(flops=flops, bytes_accessed=moved, transcendentals=0)


def pick_rows(start, w_ref, events, cols):
    base = jnp.minimum((start // 16) * 16, events - WIN)
    base = pl.multiple_of(base, 16)
    off = start - base
    row = lax.broadcasted_iota(jnp.int32, (CAP, WIN), 0)
    col = lax.broadcasted_iota(jnp.int32, (CAP, WIN), 1)
    choose = jnp.where(col == row + off, 1.0, 0.0).astype(jnp.bfloat16)
    window = w_ref[pl.ds(base, WIN), cols]
    return jnp.dot(choose, window, preferred_element_type=jnp.float32)


def pack_first(owners, bins_dev, events, starts_ref, info_ref, w_ref, out_ref):
    lines = lax.broadcasted_iota(jnp.int32, (EXTRA, 128), 0)

    def one(o, _):
        start = starts_ref[o]
        rows = pick_rows(start, w_ref, events, slice(0, COLS))
        at = jnp.minimum((start // 128) * 128, events - 256)
        at = pl.multiple_of(at, 128)
        span = pltpu.roll(info_ref[:, pl.ds(at, 256)], 256 - (start - at), 1)[:, :128]
        local = span[0:1].astype(jnp.int32) - o * bins_dev
        inside = (local >= 0) & (local < bins_dev)
        high = jnp.where(inside, local // 32, -1).astype(jnp.float32)
        low = jnp.where(inside, local % 32, 0).astype(jnp.float32)
        nominal = jnp.where(inside, span[1:2], 0.0)
        extra = jnp.where(lines == 0, high, jnp.where(lines == 1, low, jnp.where(lines == 2, nominal, 0.0)))
        out_ref[o] = jnp.concatenate([rows, extra], axis=0).astype(jnp.bfloat16)
        return 0

    lax.fori_loop(0, owners, one, 0, unroll=4)


def pack_rest(n0, n1, events, place_ref, starts_ref, w_ref, *out_refs):
    def one(z, _):
        for turn, out_ref in enumerate(out_refs):
            start = starts_ref[z * n1 + lax.rem(place_ref[0] + turn, n1)]
            rows = pick_rows(start, w_ref, events, slice(COLS, 3 * COLS)).astype(jnp.bfloat16)
            for i in range(out_ref.shape[0]):
                out_ref[i, z] = rows[:, i * COLS : (i + 1) * COLS]
        return 0

    lax.fori_loop(0, n0, one, 0)


def one_hot_of(bins_ref, at, size, bins_dev):
    ids = lax.broadcasted_iota(jnp.int32, (bins_dev, size), 0)
    return jnp.where(ids == bins_ref[:, pl.ds(at, size)], 1.0, 0.0).astype(jnp.bfloat16)


def hist_first(bins_ref, nominal_ref, background_ref, observed_ref, *refs):
    rows_refs, (out_ref, curve_ref, acc, acc_n) = refs[:-4], refs[-4:]
    bins_dev = out_ref.shape[0]
    acc[...] = jnp.zeros_like(acc)
    acc_n[...] = jnp.zeros_like(acc_n)
    size = rows_refs[0].shape[0]
    for i, rows_ref in enumerate(rows_refs):
        hot = one_hot_of(bins_ref, i * size, size, bins_dev)
        acc[...] += jnp.dot(hot, rows_ref[...], preferred_element_type=jnp.float32)
        acc_n[...] += lax.dot_general(
            hot,
            nominal_ref[:, i * size : (i + 1) * size],
            (((1,), (1,)), ((), ())),
            preferred_element_type=jnp.float32,
        )
    out_ref[...] = acc[...].astype(jnp.bfloat16)
    yields = background_ref[...] + acc_n[:, 0:1]
    curve_ref[...] = observed_ref[...] / (yields * yields)


def hist_next(bins_ref, rows_ref, out_ref, acc):
    bins_dev = out_ref.shape[0]
    acc[...] = jnp.zeros_like(acc)

    def one(i, _):
        at = pl.multiple_of(i * KB, KB)
        hot = one_hot_of(bins_ref, at, KB, bins_dev)
        acc[...] += jnp.dot(hot, rows_ref[pl.ds(at, KB), :], preferred_element_type=jnp.float32)
        return 0

    lax.fori_loop(0, rows_ref.shape[0] // KB, one, 0)
    out_ref[...] = acc[...].astype(jnp.bfloat16)


def gram(turns, curve_ref, order_ref, *refs):
    parts, out_ref = refs[:-1], refs[-1]
    chunks = len(parts) // turns
    own = jnp.concatenate([parts[c][...] for c in range(chunks)], axis=1)
    weighted = (curve_ref[...] * own.astype(jnp.float32)).astype(jnp.bfloat16)
    lhs = lax.dot_general(
        order_ref[...], weighted, (((1,), (1,)), ((), ())), preferred_element_type=jnp.float32
    ).astype(jnp.bfloat16)
    width = own.shape[1]
    step = out_ref.shape[1]
    for k in range(turns):
        partner = jnp.concatenate([parts[k * chunks + c][...] for c in range(chunks)], axis=1)
        full = jnp.dot(lhs, partner, preferred_element_type=jnp.float32).astype(jnp.bfloat16)
        for y in range(out_ref.shape[0]):
            out_ref[y, :, k * width : (k + 1) * width] = full[y * step : (y + 1) * step]


def add_across(got_ref, out_ref, wide):
    lanes = got_ref.shape[2] // 128
    total = jnp.sum(got_ref[...].astype(jnp.float32), axis=0)
    n0 = out_ref.shape[0]
    lines = total.shape[0] // n0
    wide[...] = jnp.zeros_like(wide)
    for z in range(n0):
        for j in range(lanes):
            wide[z, j * lines : (j + 1) * lines] = total[z * lines : (z + 1) * lines, j * 128 : (j + 1) * 128]
    out_ref[...] = wide[...].astype(jnp.bfloat16)


def add_along(scale, got_ref, out_ref):
    lines = out_ref.shape[0]
    total = jnp.sum(got_ref[...].astype(jnp.float32), axis=0) * scale
    for j in range(out_ref.shape[1] // 128):
        out_ref[:, j * 128 : (j + 1) * 128] = total[j * lines : (j + 1) * lines]


def from_behind(value, axis, steps):
    count = lax.axis_size(axis)
    pairs = [(source, (source + steps) % count) for source in range(count)]
    return lax.ppermute(value, axis, pairs)


def exchange(value, axis):
    return lax.all_to_all(value, axis, split_axis=0, concat_axis=0, tiled=True)


def body(event_bins, event_weights, nominal, background, observed):
    bf16, f32 = jnp.bfloat16, jnp.float32
    n0, n1 = (lax.axis_size(a) for a in BINS)
    owners = n0 * n1
    groups = lax.axis_size("params")
    events, width = event_weights.shape
    bins_dev = background.shape[0]
    chunks = width // COLS
    targets = jnp.arange(owners, dtype=jnp.int32)
    starts = jnp.sum((event_bins[None, :] < targets[:, None] * bins_dev).astype(jnp.int32), axis=1)
    info = jnp.stack([event_bins.astype(f32), nominal.astype(f32)])
    info = jnp.concatenate([info, jnp.zeros((6, events), f32)])

    slab = CAP + EXTRA
    place = lax.axis_index(BINS[1])
    send_a = pl.pallas_call(
        functools.partial(pack_first, owners, bins_dev, events),
        out_shape=jax.ShapeDtypeStruct((owners, slab, COLS), bf16),
        in_specs=[SMEM, VMEM, VMEM],
        out_specs=VMEM,
        compiler_params=PARAMS,
        cost_estimate=cost(2 * owners * CAP * WIN * COLS, 2 * owners * slab * COLS * 2),
        name="pack_first",
    )(starts, info, event_weights)
    send_b = pl.pallas_call(
        functools.partial(pack_rest, n0, n1, events),
        out_shape=[jax.ShapeDtypeStruct((chunks - 1, n0, CAP, COLS), bf16)] * n1,
        in_specs=[SMEM, SMEM, VMEM],
        out_specs=[VMEM] * n1,
        compiler_params=PARAMS,
        cost_estimate=cost(4 * owners * CAP * WIN * COLS, 4 * owners * CAP * COLS * 2),
        name="pack_rest",
    )(place.reshape(1).astype(jnp.int32), starts, event_weights)
    got_a = exchange(send_a.reshape(n0, n1 * slab, COLS), BINS[0]).reshape(n0, n1, slab, COLS)
    mid_b = [from_behind(send_b[t], BINS[1], t) if t else send_b[0] for t in range(n1)]
    got = [exchange(jnp.stack([m[i] for m in mid_b], axis=1), BINS[0]) for i in range(chunks - 1)]
    pieces = [lax.dynamic_index_in_dim(got_a, lax.rem(place + t, n1), 1, keepdims=False) for t in range(n1)]
    pieces = [from_behind(x, BINS[1], t) if t else x for t, x in enumerate(pieces)]

    extra = jnp.stack([x[:, CAP:, :CAP] for x in pieces]).astype(f32)
    local = (extra[:, :, 0] * 32.0 + extra[:, :, 1]).astype(jnp.int32)
    tail = ((0, 0), (0, 0), (0, EXTRA))
    local_wide = jnp.pad(local, tail, constant_values=-1).reshape(1, owners * slab)
    local = jnp.swapaxes(local, 0, 1).reshape(1, owners * CAP)
    nom = jnp.pad(extra[:, :, 2], tail).astype(bf16).reshape(1, owners * slab)
    nom = jnp.broadcast_to(nom, (8, owners * slab))
    tile = jax.ShapeDtypeStruct((bins_dev, COLS), bf16)
    acc = pltpu.VMEM((bins_dev, COLS), f32)
    first, curve = pl.pallas_call(
        hist_first,
        out_shape=[tile, jax.ShapeDtypeStruct((bins_dev, 1), f32)],
        in_specs=[VMEM] * (4 + n1),
        out_specs=[VMEM] * 2,
        scratch_shapes=[acc, pltpu.VMEM((bins_dev, 8), f32)],
        compiler_params=PARAMS,
        cost_estimate=cost(2 * owners * slab * bins_dev * 256, owners * slab * COLS * 2),
        name="hist_first",
    )(
        local_wide,
        nom,
        background.reshape(bins_dev, 1),
        observed.reshape(bins_dev, 1),
        *[x.reshape(n0 * slab, COLS) for x in pieces],
    )
    tiles = [first]
    for g in got:
        tiles.append(
            pl.pallas_call(
                hist_next,
                out_shape=tile,
                in_specs=[VMEM] * 2,
                out_specs=VMEM,
                scratch_shapes=[acc],
                compiler_params=PARAMS,
                cost_estimate=cost(2 * owners * CAP * bins_dev * 256, owners * CAP * COLS * 2),
                name="hist_next",
            )(local, g.reshape(owners * CAP, COLS))
        )
    turns = groups // 2 + 1
    moved = [[from_behind(t, "params", -k) if k else t for t in tiles] for k in range(turns)]

    lines = width // owners
    j = np.arange(width)
    source = ((j % (width // n1)) // lines * n1 + j // (width // n1)) * lines + j % lines
    order = np.zeros((width, width), np.float32)
    order[j, source] = 1.0
    partial = pl.pallas_call(
        functools.partial(gram, turns),
        out_shape=jax.ShapeDtypeStruct((n1, width // n1, turns * width), bf16),
        in_specs=[VMEM] * (2 + turns * chunks),
        out_specs=VMEM,
        compiler_params=PARAMS,
        cost_estimate=cost(2 * bins_dev * width * width * (turns + 1), turns * width * bins_dev * 2),
        name="gram",
    )(curve, jnp.asarray(order, bf16), *[t for row in moved for t in row])
    packed = -(-lines * turns * width // 128 // 16) * 16
    across = pl.pallas_call(
        add_across,
        out_shape=jax.ShapeDtypeStruct((n0, packed, 128), bf16),
        in_specs=[VMEM],
        out_specs=VMEM,
        scratch_shapes=[pltpu.VMEM((n0, packed, 128), f32)],
        compiler_params=PARAMS,
        name="add_across",
    )(exchange(partial, BINS[1]))
    return pl.pallas_call(
        functools.partial(add_along, 1.0 / (bins_dev * owners)),
        out_shape=jax.ShapeDtypeStruct((lines, turns * width), f32),
        in_specs=[VMEM],
        out_specs=VMEM,
        compiler_params=PARAMS,
        name="add_along",
    )(exchange(across, BINS[0]))


def solution(mesh):
    split = Mesh(mesh.devices.reshape(16, 4, mesh.shape["params"]), ("bins_0", "bins_1", "params"))
    placed = (P(BINS), P(BINS, "params"), P(BINS), P(BINS), P(BINS))
    return jax.shard_map(
        body, mesh=split, in_specs=placed, out_specs=P(PARAMS_BINS, None), check_vma=False
    )
```

```python
import functools

import jax
import jax.numpy as jnp
import numpy as np
from jax import lax
from jax.experimental import pallas as pl
from jax.experimental.pallas import tpu as pltpu
from jax.sharding import Mesh
from jax.sharding import PartitionSpec as P

BINS = ("bins_0", "bins_1")
PARAMS_BINS = ("params", "bins_0", "bins_1")
CAP = 72
EXTRA = 8
WIN = 96
COLS = 128
KB = 512
VMEM = pl.BlockSpec(memory_space=pltpu.VMEM)
SMEM = pl.BlockSpec(memory_space=pltpu.SMEM)
PARAMS = pltpu.CompilerParams(vmem_limit_bytes=24 * 2**20)


def cost(flops, moved):
    return pl.CostEstimate(flops=flops, bytes_accessed=moved, transcendentals=0)


def pick_rows(start, w_ref, events, cols):
    base = jnp.minimum((start // 16) * 16, events - WIN)
    base = pl.multiple_of(base, 16)
    off = start - base
    row = lax.broadcasted_iota(jnp.int32, (CAP, WIN), 0)
    col = lax.broadcasted_iota(jnp.int32, (CAP, WIN), 1)
    choose = jnp.where(col == row + off, 1.0, 0.0).astype(jnp.bfloat16)
    window = w_ref[pl.ds(base, WIN), cols]
    return jnp.dot(choose, window, preferred_element_type=jnp.float32)


def pack_first(owners, bins_dev, events, starts_ref, info_ref, w_ref, out_ref):
    lines = lax.broadcasted_iota(jnp.int32, (EXTRA, 128), 0)

    def one(o, _):
        start = starts_ref[o]
        rows = pick_rows(start, w_ref, events, slice(0, 2 * COLS))
        at = jnp.minimum((start // 128) * 128, events - 256)
        at = pl.multiple_of(at, 128)
        span = pltpu.roll(info_ref[:, pl.ds(at, 256)], 256 - (start - at), 1)[:, :128]
        local = span[0:1].astype(jnp.int32) - o * bins_dev
        inside = (local >= 0) & (local < bins_dev)
        high = jnp.where(inside, local // 32, -1).astype(jnp.float32)
        low = jnp.where(inside, local % 32, 0).astype(jnp.float32)
        nominal = jnp.where(inside, span[1:2], 0.0)
        extra = jnp.where(lines == 0, high, jnp.where(lines == 1, low, jnp.where(lines == 2, nominal, 0.0)))
        out_ref[o] = jnp.concatenate([rows[:, :COLS], rows[:, COLS:], extra], axis=0).astype(jnp.bfloat16)
        return 0

    lax.fori_loop(0, owners, one, 0, unroll=4)


def pack_rest(owners, events, starts_ref, w_ref, out_ref):
    def one(o, _):
        rows = pick_rows(starts_ref[o], w_ref, events, slice(2 * COLS, 3 * COLS))
        out_ref[o] = rows.astype(jnp.bfloat16)
        return 0

    lax.fori_loop(0, owners, one, 0, unroll=4)


def one_hot_of(bins_ref, at, size, bins_dev):
    ids = lax.broadcasted_iota(jnp.int32, (bins_dev, size), 0)
    return jnp.where(ids == bins_ref[:, pl.ds(at, size)], 1.0, 0.0).astype(jnp.bfloat16)


def hist_first(bins_ref, nominal_ref, background_ref, observed_ref, left_ref, right_ref, out_ref, curve_ref, acc, acc_n):
    bins_dev = out_ref.shape[0]
    acc[...] = jnp.zeros_like(acc)
    acc_n[...] = jnp.zeros_like(acc_n)

    def one(i, _):
        at = pl.multiple_of(i * KB, KB)
        hot = one_hot_of(bins_ref, at, KB, bins_dev)
        rows = jnp.concatenate([left_ref[pl.ds(at, KB), :], right_ref[pl.ds(at, KB), :]], axis=1)
        acc[...] += jnp.dot(hot, rows, preferred_element_type=jnp.float32)
        acc_n[...] += lax.dot_general(
            hot, nominal_ref[:, pl.ds(at, KB)], (((1,), (1,)), ((), ())), preferred_element_type=jnp.float32
        )
        return 0

    lax.fori_loop(0, left_ref.shape[0] // KB, one, 0)
    out_ref[...] = acc[...].astype(jnp.bfloat16)
    yields = background_ref[...] + acc_n[:, 0:1]
    curve_ref[...] = observed_ref[...] / (yields * yields)


def hist_next(bins_ref, rows_ref, out_ref, acc):
    bins_dev = out_ref.shape[0]
    acc[...] = jnp.zeros_like(acc)

    def one(i, _):
        at = pl.multiple_of(i * KB, KB)
        hot = one_hot_of(bins_ref, at, KB, bins_dev)
        acc[...] += jnp.dot(hot, rows_ref[pl.ds(at, KB), :], preferred_element_type=jnp.float32)
        return 0

    lax.fori_loop(0, rows_ref.shape[0] // KB, one, 0)
    out_ref[...] = acc[...].astype(jnp.bfloat16)


def gram(turns, curve_ref, order_ref, *refs):
    parts, out_ref = refs[:-1], refs[-1]
    chunks = len(parts) // turns
    own = jnp.concatenate([parts[c][...] for c in range(chunks)], axis=1)
    weighted = (curve_ref[...] * own.astype(jnp.float32)).astype(jnp.bfloat16)
    lhs = lax.dot_general(
        order_ref[...], weighted, (((1,), (1,)), ((), ())), preferred_element_type=jnp.float32
    ).astype(jnp.bfloat16)
    width = own.shape[1]
    step = out_ref.shape[1]
    for k in range(turns):
        partner = jnp.concatenate([parts[k * chunks + c][...] for c in range(chunks)], axis=1)
        full = jnp.dot(lhs, partner, preferred_element_type=jnp.float32).astype(jnp.bfloat16)
        for y in range(out_ref.shape[0]):
            out_ref[y, :, k * width : (k + 1) * width] = full[y * step : (y + 1) * step]


def add_across(got_ref, out_ref, wide):
    lanes = got_ref.shape[2] // 128
    total = jnp.sum(got_ref[...].astype(jnp.float32), axis=0)
    n0 = out_ref.shape[0]
    lines = total.shape[0] // n0
    wide[...] = jnp.zeros_like(wide)
    for z in range(n0):
        for j in range(lanes):
            wide[z, j * lines : (j + 1) * lines] = total[z * lines : (z + 1) * lines, j * 128 : (j + 1) * 128]
    out_ref[...] = wide[...].astype(jnp.bfloat16)


def add_along(scale, got_ref, out_ref):
    lines = out_ref.shape[0]
    total = jnp.sum(got_ref[...].astype(jnp.float32), axis=0) * scale
    for j in range(out_ref.shape[1] // 128):
        out_ref[:, j * 128 : (j + 1) * 128] = total[j * lines : (j + 1) * lines]


def from_behind(value, axis, steps):
    count = lax.axis_size(axis)
    pairs = [(source, (source + steps) % count) for source in range(count)]
    return lax.ppermute(value, axis, pairs)


def exchange(value, axis):
    return lax.all_to_all(value, axis, split_axis=0, concat_axis=0, tiled=True)


def body(event_bins, event_weights, nominal, background, observed):
    bf16, f32 = jnp.bfloat16, jnp.float32
    n0, n1 = (lax.axis_size(a) for a in BINS)
    owners = n0 * n1
    groups = lax.axis_size("params")
    events, width = event_weights.shape
    bins_dev = background.shape[0]
    targets = jnp.arange(owners, dtype=jnp.int32)
    starts = jnp.sum((event_bins[None, :] < targets[:, None] * bins_dev).astype(jnp.int32), axis=1)
    info = jnp.stack([event_bins.astype(f32), nominal.astype(f32)])
    info = jnp.concatenate([info, jnp.zeros((6, events), f32)])

    slab = 2 * CAP + EXTRA
    send_a = pl.pallas_call(
        functools.partial(pack_first, owners, bins_dev, events),
        out_shape=jax.ShapeDtypeStruct((owners, slab, COLS), bf16),
        in_specs=[SMEM, VMEM, VMEM],
        out_specs=VMEM,
        compiler_params=PARAMS,
        cost_estimate=cost(4 * owners * CAP * WIN * COLS, 2 * owners * slab * COLS * 2),
        name="pack_first",
    )(starts, info, event_weights)
    got_a = exchange(send_a, BINS)
    send_b = pl.pallas_call(
        functools.partial(pack_rest, owners, events),
        out_shape=jax.ShapeDtypeStruct((owners, CAP, COLS), bf16),
        in_specs=[SMEM, VMEM],
        out_specs=VMEM,
        compiler_params=PARAMS,
        cost_estimate=cost(2 * owners * CAP * WIN * COLS, 2 * owners * CAP * COLS * 2),
        name="pack_rest",
    )(starts, event_weights)
    send_b, got_a = lax.optimization_barrier((send_b, got_a))
    got_b = exchange(send_b, BINS)

    total = owners * CAP
    extra = got_a[:, 2 * CAP :, :CAP].astype(f32)
    local = (extra[:, 0] * 32.0 + extra[:, 1]).astype(jnp.int32).reshape(1, total)
    nom = jnp.broadcast_to(extra[:, 2].astype(bf16).reshape(1, total), (8, total))
    left, right = (got_a[:, i * CAP : (i + 1) * CAP].reshape(total, COLS) for i in range(2))
    first, curve = pl.pallas_call(
        hist_first,
        out_shape=[jax.ShapeDtypeStruct((bins_dev, 2 * COLS), bf16), jax.ShapeDtypeStruct((bins_dev, 1), f32)],
        in_specs=[VMEM] * 6,
        out_specs=[VMEM] * 2,
        scratch_shapes=[pltpu.VMEM((bins_dev, 2 * COLS), f32), pltpu.VMEM((bins_dev, 8), f32)],
        compiler_params=PARAMS,
        cost_estimate=cost(2 * total * bins_dev * 512, 2 * total * COLS * 2),
        name="hist_first",
    )(local, nom, background.reshape(bins_dev, 1), observed.reshape(bins_dev, 1), left, right)
    last = pl.pallas_call(
        hist_next,
        out_shape=jax.ShapeDtypeStruct((bins_dev, COLS), bf16),
        in_specs=[VMEM] * 2,
        out_specs=VMEM,
        scratch_shapes=[pltpu.VMEM((bins_dev, COLS), f32)],
        compiler_params=PARAMS,
        cost_estimate=cost(2 * total * bins_dev * 256, total * COLS * 2),
        name="hist_next",
    )(local, got_b.reshape(total, COLS))
    tiles = [first, last]
    chunks = len(tiles)
    turns = groups // 2 + 1
    moved = [[from_behind(t, "params", -k) if k else t for t in tiles] for k in range(turns)]

    lines = width // owners
    j = np.arange(width)
    source = ((j % (width // n1)) // lines * n1 + j // (width // n1)) * lines + j % lines
    order = np.zeros((width, width), np.float32)
    order[j, source] = 1.0
    partial = pl.pallas_call(
        functools.partial(gram, turns),
        out_shape=jax.ShapeDtypeStruct((n1, width // n1, turns * width), bf16),
        in_specs=[VMEM] * (2 + turns * chunks),
        out_specs=VMEM,
        compiler_params=PARAMS,
        cost_estimate=cost(2 * bins_dev * width * width * (turns + 1), turns * width * bins_dev * 2),
        name="gram",
    )(curve, jnp.asarray(order, bf16), *[t for row in moved for t in row])
    packed = -(-lines * turns * width // 128 // 16) * 16
    across = pl.pallas_call(
        add_across,
        out_shape=jax.ShapeDtypeStruct((n0, packed, 128), bf16),
        in_specs=[VMEM],
        out_specs=VMEM,
        scratch_shapes=[pltpu.VMEM((n0, packed, 128), f32)],
        compiler_params=PARAMS,
        name="add_across",
    )(exchange(partial, BINS[1]))
    return pl.pallas_call(
        functools.partial(add_along, 1.0 / (bins_dev * owners)),
        out_shape=jax.ShapeDtypeStruct((lines, turns * width), f32),
        in_specs=[VMEM],
        out_specs=VMEM,
        compiler_params=PARAMS,
        name="add_along",
    )(exchange(across, BINS[0]))


def solution(mesh):
    split = Mesh(mesh.devices.reshape(16, 4, mesh.shape["params"]), ("bins_0", "bins_1", "params"))
    placed = (P(BINS), P(BINS, "params"), P(BINS), P(BINS), P(BINS))
    return jax.shard_map(
        body, mesh=split, in_specs=placed, out_specs=P(PARAMS_BINS, None), check_vma=False
    )
```

```python
import functools

import jax
import jax.numpy as jnp
import numpy as np
from jax import lax
from jax.experimental import pallas as pl
from jax.experimental.pallas import tpu as pltpu
from jax.sharding import Mesh
from jax.sharding import PartitionSpec as P

BINS = ("bins_0", "bins_1")
PARAMS_BINS = ("params", "bins_0", "bins_1")
CAP = 72
EXTRA = 8
COLS = 128
KB = 512
VMEM = pl.BlockSpec(memory_space=pltpu.VMEM)
SMEM = pl.BlockSpec(memory_space=pltpu.SMEM)
PARAMS = pltpu.CompilerParams(vmem_limit_bytes=24 * 2**20)
SMALL_PARAMS = pltpu.CompilerParams(vmem_limit_bytes=12 * 2**20)
F32 = jnp.float32
BF16 = jnp.bfloat16


def cost(flops, moved):
    return pl.CostEstimate(flops=flops, bytes_accessed=moved, transcendentals=0)


def dot(a, b):
    return jnp.dot(a, b, preferred_element_type=F32)


def dot_t(a, b):
    return lax.dot_general(a, b, (((1,), (1,)), ((), ())), preferred_element_type=F32)


def spread(w_ref, turn_ref, tiles):
    events = w_ref.shape[0]
    step = 512 if events % 512 == 0 else events

    def one(i, _):
        at = pl.multiple_of(i * step, step)
        rows = dot(w_ref[pl.ds(at, step), :], turn_ref[...])
        for t, tile in enumerate(tiles):
            tile[pl.ds(at, step), :] = rows[:, t * COLS : (t + 1) * COLS]
        return 0

    lax.fori_loop(0, events // step, one, 0)
    for tile in tiles:
        tile[events:, :] = jnp.zeros((tile.shape[0] - events, COLS), F32)


def pack_first(owners, bins_dev, events, starts_ref, info_ref, w_ref, turn_ref, out_ref, left, right):
    lines = lax.broadcasted_iota(jnp.int32, (EXTRA, 128), 0)
    spread(w_ref, turn_ref, (left, right))

    def one(o, _):
        start = starts_ref[o]
        at = jnp.minimum((start // 128) * 128, events - 256)
        at = pl.multiple_of(at, 128)
        span = pltpu.roll(info_ref[:, pl.ds(at, 256)], 256 - (start - at), 1)[:, :128]
        local = span[0:1].astype(jnp.int32) - o * bins_dev
        inside = (local >= 0) & (local < bins_dev)
        high = jnp.where(inside, local // 32, -1).astype(F32)
        low = jnp.where(inside, local % 32, 0).astype(F32)
        nominal = jnp.where(inside, span[1:2], 0.0)
        extra = jnp.where(lines == 0, high, jnp.where(lines == 1, low, jnp.where(lines == 2, nominal, 0.0)))
        rows = [tile[pl.ds(start, CAP), :] for tile in (left, right)]
        out_ref[o] = jnp.concatenate([*rows, extra], axis=0).astype(BF16)
        return 0

    lax.fori_loop(0, owners, one, 0, unroll=4)


def pack_rest(owners, starts_ref, w_ref, turn_ref, out_ref, tile):
    spread(w_ref, turn_ref, (tile,))

    def one(o, _):
        out_ref[o] = tile[pl.ds(starts_ref[o], CAP), :].astype(BF16)
        return 0

    lax.fori_loop(0, owners, one, 0, unroll=4)


def one_hot_of(bins_ref, at, size, bins_dev):
    ids = lax.broadcasted_iota(jnp.int32, (bins_dev, size), 0)
    return jnp.where(ids == bins_ref[:, pl.ds(at, size)], 1.0, 0.0).astype(BF16)


def hist_first(bins_ref, nominal_ref, background_ref, observed_ref, left_ref, right_ref, out_ref, curve_ref, acc, acc_n):
    bins_dev = out_ref.shape[0]
    acc[...] = jnp.zeros_like(acc)
    acc_n[...] = jnp.zeros_like(acc_n)

    def one(i, _):
        at = pl.multiple_of(i * KB, KB)
        hot = one_hot_of(bins_ref, at, KB, bins_dev)
        rows = jnp.concatenate([left_ref[pl.ds(at, KB), :], right_ref[pl.ds(at, KB), :]], axis=1)
        acc[...] += dot(hot, rows)
        acc_n[...] += dot_t(hot, nominal_ref[:, pl.ds(at, KB)])
        return 0

    lax.fori_loop(0, left_ref.shape[0] // KB, one, 0)
    out_ref[...] = acc[...].astype(BF16)
    yields = background_ref[...] + acc_n[:, 0:1]
    curve_ref[...] = observed_ref[...] / (yields * yields)


def hist_next(bins_ref, rows_ref, out_ref, acc):
    bins_dev = out_ref.shape[0]
    acc[...] = jnp.zeros_like(acc)

    def one(i, _):
        at = pl.multiple_of(i * KB, KB)
        hot = one_hot_of(bins_ref, at, KB, bins_dev)
        acc[...] += dot(hot, rows_ref[pl.ds(at, KB), :])
        return 0

    lax.fori_loop(0, rows_ref.shape[0] // KB, one, 0)
    out_ref[...] = acc[...].astype(BF16)


def left_side(curve_ref, own_ref):
    weighted = (curve_ref[...] * own_ref[...].astype(F32)).astype(BF16)
    size = weighted.shape[1]
    row = lax.broadcasted_iota(jnp.int32, (size, size), 0)
    col = lax.broadcasted_iota(jnp.int32, (size, size), 1)
    return dot_t(jnp.where(row == col, 1.0, 0.0).astype(BF16), weighted).astype(BF16)


def gram_early(curve_ref, *refs):
    parts, out_ref = refs[:-1], refs[-1]
    n1, step, _ = out_ref.shape
    lhs = left_side(curve_ref, parts[0])
    wide = 2 * COLS
    for k, part in enumerate(parts):
        full = dot(lhs, part[...]).astype(BF16)
        for y in range(n1):
            out_ref[y, :, k * wide : (k + 1) * wide] = full[y * step : (y + 1) * step]


def gram_late(turns, curve_ref, *refs):
    first, last, out_ref = refs[:turns], refs[turns:-1], refs[-1]
    n1 = out_ref.shape[0]
    lhs_a = left_side(curve_ref, first[0])
    lhs_b = left_side(curve_ref, last[0])
    for k in range(turns):
        partner = last[k][...]
        side = dot(lhs_a, partner).astype(BF16)
        low = jnp.concatenate([dot(lhs_b, first[k][...]), dot(lhs_b, partner)], axis=1).astype(BF16)
        sa, sb = side.shape[0] // n1, low.shape[0] // n1
        for y in range(n1):
            out_ref[y, k * sa : (k + 1) * sa] = side[y * sa : (y + 1) * sa]
            for t in range(3):
                at = turns * sa + (3 * k + t) * sb
                out_ref[y, at : at + sb] = low[y * sb : (y + 1) * sb, t * COLS : (t + 1) * COLS]


def add_across(turns, early_ref, late_ref, turn_ref, out_ref, wide):
    n0 = out_ref.shape[0]
    early = jnp.sum(early_ref[...].astype(F32), axis=0).astype(BF16)
    late = jnp.sum(late_ref[...].astype(F32), axis=0).astype(BF16)
    sa = early.shape[0]
    sb = sa // 2
    la, lb = sa // n0, sb // n0
    lines = la + lb
    wide[...] = jnp.zeros_like(wide)
    for k in range(turns):
        high = jnp.concatenate(
            [early[:, 2 * k * COLS : 2 * (k + 1) * COLS], late[k * sa : (k + 1) * sa]], axis=1
        )
        at = turns * sa + 3 * k * sb
        low = jnp.concatenate([late[at + t * sb : at + (t + 1) * sb] for t in range(3)], axis=1)
        high = dot_t(high, turn_ref[...])
        low = dot_t(low, turn_ref[...])
        for t in range(3):
            lanes = slice(t * COLS, (t + 1) * COLS)
            for z in range(n0):
                at = (3 * k + t) * lines
                wide[z, at : at + la] = high[z * la : (z + 1) * la, lanes]
                wide[z, at + la : at + lines] = low[z * lb : (z + 1) * lb, lanes]
    out_ref[...] = wide[...].astype(BF16)


def add_along(scale, got_ref, out_ref):
    lines = out_ref.shape[0]
    total = jnp.sum(got_ref[...].astype(F32), axis=0) * scale
    for j in range(out_ref.shape[1] // 128):
        out_ref[:, j * 128 : (j + 1) * 128] = total[j * lines : (j + 1) * lines]


def from_behind(value, axis, steps):
    count = lax.axis_size(axis)
    pairs = [(source, (source + steps) % count) for source in range(count)]
    return lax.ppermute(value, axis, pairs)


def exchange(value, axis):
    return lax.all_to_all(value, axis, split_axis=0, concat_axis=0, tiled=True)


def column_order(n0, n1, width):
    lines = width // (n0 * n1)
    la = 2 * lines // 3
    m = np.arange(width)
    owner, r = m // lines, m % lines
    rank = (owner % n1) * n0 + owner // n1
    place = np.where(r < la, rank * la + r, n0 * n1 * la + rank * (lines - la) + r - la)
    turn = np.zeros((width, width), np.float32)
    turn[m, place] = 1.0
    return turn


def body(event_bins, event_weights, nominal, background, observed):
    n0, n1 = (lax.axis_size(a) for a in BINS)
    owners = n0 * n1
    groups = lax.axis_size("params")
    events, width = event_weights.shape
    bins_dev = background.shape[0]
    turns = groups // 2 + 1
    lines = width // owners
    turn = column_order(n0, n1, width)
    targets = jnp.arange(owners, dtype=jnp.int32)
    starts = jnp.sum((event_bins[None, :] < targets[:, None] * bins_dev).astype(jnp.int32), axis=1)
    info = jnp.stack([event_bins.astype(F32), nominal.astype(F32)])
    info = jnp.concatenate([info, jnp.zeros((6, events), F32)])

    slab = 2 * CAP + EXTRA
    scratch = pltpu.VMEM((events + CAP, COLS), F32)
    send_a = pl.pallas_call(
        functools.partial(pack_first, owners, bins_dev, events),
        out_shape=jax.ShapeDtypeStruct((owners, slab, COLS), BF16),
        in_specs=[SMEM, VMEM, VMEM, VMEM],
        out_specs=VMEM,
        scratch_shapes=[scratch, scratch],
        compiler_params=PARAMS,
        cost_estimate=cost(2 * events * width * 2 * COLS, 2 * owners * slab * COLS * 2),
        name="pack_first",
    )(starts, info, event_weights, jnp.asarray(turn[:, : 2 * COLS], BF16))
    got_a = exchange(send_a, BINS)
    send_b = pl.pallas_call(
        functools.partial(pack_rest, owners),
        out_shape=jax.ShapeDtypeStruct((owners, CAP, COLS), BF16),
        in_specs=[SMEM, VMEM, VMEM],
        out_specs=VMEM,
        scratch_shapes=[scratch],
        compiler_params=PARAMS,
        cost_estimate=cost(2 * events * width * COLS, 2 * owners * CAP * COLS * 2),
        name="pack_rest",
    )(starts, event_weights, jnp.asarray(turn[:, 2 * COLS :], BF16))
    send_b, got_a = lax.optimization_barrier((send_b, got_a))
    got_b = exchange(send_b, BINS)

    total = owners * CAP
    extra = got_a[:, 2 * CAP :, :CAP].astype(F32)
    local = (extra[:, 0] * 32.0 + extra[:, 1]).astype(jnp.int32).reshape(1, total)
    nom = jnp.broadcast_to(extra[:, 2].astype(BF16).reshape(1, total), (8, total))
    left, right = (got_a[:, i * CAP : (i + 1) * CAP].reshape(total, COLS) for i in range(2))
    first, curve = pl.pallas_call(
        hist_first,
        out_shape=[jax.ShapeDtypeStruct((bins_dev, 2 * COLS), BF16), jax.ShapeDtypeStruct((bins_dev, 1), F32)],
        in_specs=[VMEM] * 6,
        out_specs=[VMEM] * 2,
        scratch_shapes=[pltpu.VMEM((bins_dev, 2 * COLS), F32), pltpu.VMEM((bins_dev, 8), F32)],
        compiler_params=SMALL_PARAMS,
        cost_estimate=cost(2 * total * bins_dev * 512, 2 * total * COLS * 2),
        name="hist_first",
    )(local, nom, background.reshape(bins_dev, 1), observed.reshape(bins_dev, 1), left, right)
    firsts = [first] + [from_behind(first, "params", -k) for k in range(1, turns)]
    early = pl.pallas_call(
        gram_early,
        out_shape=jax.ShapeDtypeStruct((n1, 2 * COLS // n1, turns * 2 * COLS), BF16),
        in_specs=[VMEM] * (1 + turns),
        out_specs=VMEM,
        compiler_params=SMALL_PARAMS,
        cost_estimate=cost(2 * bins_dev * 4 * COLS * COLS * (turns + 1), 2 * turns * COLS * bins_dev * 2),
        name="gram_early",
    )(curve, *firsts)
    early, got_b = lax.optimization_barrier((early, got_b))
    early = exchange(early, BINS[1])

    last = pl.pallas_call(
        hist_next,
        out_shape=jax.ShapeDtypeStruct((bins_dev, COLS), BF16),
        in_specs=[VMEM] * 2,
        out_specs=VMEM,
        scratch_shapes=[pltpu.VMEM((bins_dev, COLS), F32)],
        compiler_params=SMALL_PARAMS,
        cost_estimate=cost(2 * total * bins_dev * 256, total * COLS * 2),
        name="hist_next",
    )(local, got_b.reshape(total, COLS))
    lasts = [last] + [from_behind(last, "params", -k) for k in range(1, turns)]
    rows_late = turns * (2 * COLS + 3 * COLS) // n1
    late = pl.pallas_call(
        functools.partial(gram_late, turns),
        out_shape=jax.ShapeDtypeStruct((n1, rows_late, COLS), BF16),
        in_specs=[VMEM] * (1 + 2 * turns),
        out_specs=VMEM,
        compiler_params=SMALL_PARAMS,
        cost_estimate=cost(2 * bins_dev * 5 * COLS * COLS * (turns + 1), 3 * turns * COLS * bins_dev * 2),
        name="gram_late",
    )(curve, *firsts, *lasts)
    late = exchange(late, BINS[1])

    packed = -(-lines * turns * width // 128 // 16) * 16
    across = pl.pallas_call(
        functools.partial(add_across, turns),
        out_shape=jax.ShapeDtypeStruct((n0, packed, 128), BF16),
        in_specs=[VMEM] * 3,
        out_specs=VMEM,
        scratch_shapes=[pltpu.VMEM((n0, packed, 128), F32)],
        compiler_params=SMALL_PARAMS,
        name="add_across",
    )(early, late, jnp.asarray(turn, BF16))
    return pl.pallas_call(
        functools.partial(add_along, 1.0 / (bins_dev * owners)),
        out_shape=jax.ShapeDtypeStruct((lines, turns * width), F32),
        in_specs=[VMEM],
        out_specs=VMEM,
        compiler_params=SMALL_PARAMS,
        name="add_along",
    )(exchange(across, BINS[0]))


def solution(mesh):
    split = Mesh(mesh.devices.reshape(16, 4, mesh.shape["params"]), ("bins_0", "bins_1", "params"))
    placed = (P(BINS), P(BINS, "params"), P(BINS), P(BINS), P(BINS))
    return jax.shard_map(
        body, mesh=split, in_specs=placed, out_specs=P(PARAMS_BINS, None), check_vma=False
    )
```

```python
import functools

import jax
import jax.numpy as jnp
import numpy as np
from jax import lax
from jax.experimental import pallas as pl
from jax.experimental.pallas import tpu as pltpu
from jax.sharding import Mesh
from jax.sharding import PartitionSpec as P

BINS = ("bins_0", "bins_1")
PARAMS_BINS = ("params", "bins_0", "bins_1")
CAP = 72
EXTRA = 8
WIN = 96
COLS = 128
KB = 512
VMEM = pl.BlockSpec(memory_space=pltpu.VMEM)
SMEM = pl.BlockSpec(memory_space=pltpu.SMEM)
PARAMS = pltpu.CompilerParams(vmem_limit_bytes=24 * 2**20)


def cost(flops, moved):
    return pl.CostEstimate(flops=flops, bytes_accessed=moved, transcendentals=0)


def pick_rows(start, w_ref, events, cols):
    base = jnp.minimum((start // 16) * 16, events - WIN)
    base = pl.multiple_of(base, 16)
    off = start - base
    row = lax.broadcasted_iota(jnp.int32, (CAP, WIN), 0)
    col = lax.broadcasted_iota(jnp.int32, (CAP, WIN), 1)
    choose = jnp.where(col == row + off, 1.0, 0.0).astype(jnp.bfloat16)
    window = w_ref[pl.ds(base, WIN), cols]
    return jnp.dot(choose, window, preferred_element_type=jnp.float32)


def lanes_from(ref, start):
    line = start // 128
    after = jnp.minimum(line + 1, ref.shape[0] - 1)
    off = start - line * 128
    back = lax.rem(128 - off, 128)
    lane = lax.broadcasted_iota(jnp.int32, (1, 128), 1)
    here = pltpu.roll(ref[pl.ds(line, 1), :], back, 1)
    there = pltpu.roll(ref[pl.ds(after, 1), :], back, 1)
    return jnp.where(lane < 128 - off, here, there)


def pack_first(owners, bins_dev, starts_ref, bins_ref, nominal_ref, w_ref, out_ref):
    events = w_ref.shape[0]
    lines = lax.broadcasted_iota(jnp.int32, (EXTRA, 128), 0)

    def one(o, _):
        start = starts_ref[o]
        rows = pick_rows(start, w_ref, events, slice(0, 2 * COLS))
        local = lanes_from(bins_ref, start) - o * bins_dev
        inside = (local >= 0) & (local < bins_dev)
        high = jnp.where(inside, local >> 5, -1).astype(jnp.float32)
        low = jnp.where(inside, local & 31, 0).astype(jnp.float32)
        nominal = jnp.where(inside, lanes_from(nominal_ref, start), 0.0)
        extra = jnp.where(lines == 0, high, jnp.where(lines == 1, low, jnp.where(lines == 2, nominal, 0.0)))
        out_ref[o] = jnp.concatenate([rows[:, :COLS], rows[:, COLS:], extra], axis=0).astype(jnp.bfloat16)
        return 0

    lax.fori_loop(0, owners, one, 0, unroll=8)


def pack_rest(n0, n1, place_ref, starts_ref, w_ref, *out_refs):
    events = w_ref.shape[0]

    def one(z, _):
        for turn, out_ref in enumerate(out_refs):
            start = starts_ref[z * n1 + lax.rem(place_ref[0] + turn, n1)]
            out_ref[z] = pick_rows(start, w_ref, events, slice(2 * COLS, 3 * COLS)).astype(jnp.bfloat16)
        return 0

    lax.fori_loop(0, n0, one, 0, unroll=2)


def one_hot_of(bins_ref, at, size, bins_dev):
    ids = lax.broadcasted_iota(jnp.int32, (bins_dev, size), 0)
    return jnp.where(ids == bins_ref[:, pl.ds(at, size)], 1.0, 0.0).astype(jnp.bfloat16)


def hist_first(bins_ref, nominal_ref, background_ref, observed_ref, left_ref, right_ref, out_ref, curve_ref, acc, acc_n):
    bins_dev = out_ref.shape[0]
    acc[...] = jnp.zeros_like(acc)
    acc_n[...] = jnp.zeros_like(acc_n)

    def one(i, _):
        at = pl.multiple_of(i * KB, KB)
        hot = one_hot_of(bins_ref, at, KB, bins_dev)
        rows = jnp.concatenate([left_ref[pl.ds(at, KB), :], right_ref[pl.ds(at, KB), :]], axis=1)
        acc[...] += jnp.dot(hot, rows, preferred_element_type=jnp.float32)
        acc_n[...] += lax.dot_general(
            hot, nominal_ref[:, pl.ds(at, KB)], (((1,), (1,)), ((), ())), preferred_element_type=jnp.float32
        )
        return 0

    lax.fori_loop(0, left_ref.shape[0] // KB, one, 0)
    out_ref[...] = acc[...].astype(jnp.bfloat16)
    yields = background_ref[...] + acc_n[:, 0:1]
    curve_ref[...] = observed_ref[...] / (yields * yields)


def hist_next(bins_ref, rows_ref, out_ref, acc):
    bins_dev = out_ref.shape[0]
    acc[...] = jnp.zeros_like(acc)

    def one(i, _):
        at = pl.multiple_of(i * KB, KB)
        hot = one_hot_of(bins_ref, at, KB, bins_dev)
        acc[...] += jnp.dot(hot, rows_ref[pl.ds(at, KB), :], preferred_element_type=jnp.float32)
        return 0

    lax.fori_loop(0, rows_ref.shape[0] // KB, one, 0)
    out_ref[...] = acc[...].astype(jnp.bfloat16)


def left_side(curve_ref, order_ref, first_ref, last_ref):
    own = jnp.concatenate([first_ref[...], last_ref[...]], axis=1)
    weighted = (curve_ref[...] * own.astype(jnp.float32)).astype(jnp.bfloat16)
    return lax.dot_general(
        order_ref[...], weighted, (((1,), (1,)), ((), ())), preferred_element_type=jnp.float32
    ).astype(jnp.bfloat16)


def gram_first(curve_ref, order_ref, last_ref, *refs):
    firsts, (out_ref, lhs_ref) = refs[:-2], refs[-2:]
    lhs = left_side(curve_ref, order_ref, firsts[0], last_ref)
    lhs_ref[...] = lhs
    wide, step = firsts[0].shape[1], out_ref.shape[1]
    for k, part in enumerate(firsts):
        full = jnp.dot(lhs, part[...], preferred_element_type=jnp.float32).astype(jnp.bfloat16)
        for y in range(out_ref.shape[0]):
            out_ref[y, :, k * wide : (k + 1) * wide] = full[y * step : (y + 1) * step]


def gram_last(lhs_ref, *refs):
    lasts, out_ref = refs[:-1], refs[-1]
    lhs = lhs_ref[...]
    wide, step = lasts[0].shape[1], out_ref.shape[1]
    for k, part in enumerate(lasts):
        full = jnp.dot(lhs, part[...], preferred_element_type=jnp.float32).astype(jnp.bfloat16)
        for y in range(out_ref.shape[0]):
            out_ref[y, :, k * wide : (k + 1) * wide] = full[y * step : (y + 1) * step]


def add_across(turns, first_ref, last_ref, out_ref, wide):
    n0 = out_ref.shape[0]
    lines = first_ref.shape[1] // n0
    first = jnp.sum(first_ref[...].astype(jnp.float32), axis=0)
    last = jnp.sum(last_ref[...].astype(jnp.float32), axis=0)
    wide[...] = jnp.zeros_like(wide)
    for k in range(turns):
        for t in range(3):
            tile, at = (last, k * COLS) if t == 2 else (first, (2 * k + t) * COLS)
            tile = tile[:, at : at + COLS]
            at = (3 * k + t) * lines
            for z in range(n0):
                wide[z, at : at + lines] = tile[z * lines : (z + 1) * lines]
    out_ref[...] = wide[...].astype(jnp.bfloat16)


def add_along(scale, got_ref, out_ref):
    lines = out_ref.shape[0]
    total = jnp.sum(got_ref[...].astype(jnp.float32), axis=0) * scale
    for j in range(out_ref.shape[1] // 128):
        out_ref[:, j * 128 : (j + 1) * 128] = total[j * lines : (j + 1) * lines]


def from_behind(value, axis, steps):
    count = lax.axis_size(axis)
    pairs = [(source, (source + steps) % count) for source in range(count)]
    return lax.ppermute(value, axis, pairs)


def exchange(value, axis):
    return lax.all_to_all(value, axis, split_axis=0, concat_axis=0, tiled=True)


def body(event_bins, event_weights, nominal, background, observed):
    bf16, f32 = jnp.bfloat16, jnp.float32
    n0, n1 = (lax.axis_size(a) for a in BINS)
    owners = n0 * n1
    groups = lax.axis_size("params")
    events, width = event_weights.shape
    bins_dev = background.shape[0]
    targets = jnp.arange(owners, dtype=jnp.int32)
    starts = jnp.sum((event_bins[None, :] < targets[:, None] * bins_dev).astype(jnp.int32), axis=1)
    place = lax.axis_index(BINS[1])
    slab = 2 * CAP + EXTRA
    send_a = pl.pallas_call(
        functools.partial(pack_first, owners, bins_dev),
        out_shape=jax.ShapeDtypeStruct((owners, slab, COLS), bf16),
        in_specs=[SMEM, VMEM, VMEM, VMEM],
        out_specs=VMEM,
        compiler_params=PARAMS,
        cost_estimate=cost(4 * owners * CAP * WIN * COLS, 2 * owners * slab * COLS * 2),
        name="pack_first",
    )(starts, event_bins.reshape(-1, 128), nominal.astype(f32).reshape(-1, 128), event_weights)
    got_a = exchange(send_a, BINS)
    sends = pl.pallas_call(
        functools.partial(pack_rest, n0, n1),
        out_shape=[jax.ShapeDtypeStruct((n0, CAP, COLS), bf16)] * n1,
        in_specs=[SMEM, SMEM, VMEM],
        out_specs=[VMEM] * n1,
        compiler_params=PARAMS,
        cost_estimate=cost(2 * owners * CAP * WIN * COLS, 2 * owners * CAP * COLS * 2),
        name="pack_rest",
    )(place.reshape(1).astype(jnp.int32), starts, event_weights)
    mid = jnp.stack([from_behind(x, BINS[1], t) if t else x for t, x in enumerate(sends)], axis=1)
    mid, got_a = lax.optimization_barrier((mid, got_a))
    got_b = exchange(mid, BINS[0])

    total = owners * CAP
    extra = got_a[:, 2 * CAP :, :CAP].astype(f32)
    local = (extra[:, 0] * 32.0 + extra[:, 1]).astype(jnp.int32)
    back = local.reshape(n0, n1, CAP)[:, ::-1]
    local_b = lax.dynamic_slice_in_dim(jnp.concatenate([back, back], axis=1), n1 - 1 - place, n1, axis=1)
    local_b = local_b.reshape(1, total)
    local = local.reshape(1, total)
    nom = jnp.broadcast_to(extra[:, 2].astype(bf16).reshape(1, total), (8, total))
    left, right = (got_a[:, i * CAP : (i + 1) * CAP].reshape(total, COLS) for i in range(2))
    first, curve = pl.pallas_call(
        hist_first,
        out_shape=[jax.ShapeDtypeStruct((bins_dev, 2 * COLS), bf16), jax.ShapeDtypeStruct((bins_dev, 1), f32)],
        in_specs=[VMEM] * 6,
        out_specs=[VMEM] * 2,
        scratch_shapes=[pltpu.VMEM((bins_dev, 2 * COLS), f32), pltpu.VMEM((bins_dev, 8), f32)],
        compiler_params=PARAMS,
        cost_estimate=cost(2 * total * bins_dev * 512, 2 * total * COLS * 2),
        name="hist_first",
    )(local, nom, background.reshape(bins_dev, 1), observed.reshape(bins_dev, 1), left, right)
    last = pl.pallas_call(
        hist_next,
        out_shape=jax.ShapeDtypeStruct((bins_dev, COLS), bf16),
        in_specs=[VMEM] * 2,
        out_specs=VMEM,
        scratch_shapes=[pltpu.VMEM((bins_dev, COLS), f32)],
        compiler_params=PARAMS,
        cost_estimate=cost(2 * total * bins_dev * 256, total * COLS * 2),
        name="hist_next",
    )(local_b, got_b.reshape(total, COLS))
    turns = groups // 2 + 1
    firsts = [from_behind(first, "params", -k) if k else first for k in range(turns)]
    lasts = [from_behind(last, "params", -k) if k else last for k in range(turns)]

    lines = width // owners
    j = np.arange(width)
    source = ((j % (width // n1)) // lines * n1 + j // (width // n1)) * lines + j % lines
    order = np.zeros((width, width), np.float32)
    order[j, source] = 1.0
    part_a, lhs = pl.pallas_call(
        gram_first,
        out_shape=[
            jax.ShapeDtypeStruct((n1, width // n1, turns * 2 * COLS), bf16),
            jax.ShapeDtypeStruct((width, bins_dev), bf16),
        ],
        in_specs=[VMEM] * (3 + turns),
        out_specs=[VMEM] * 2,
        compiler_params=PARAMS,
        cost_estimate=cost(2 * bins_dev * width * 2 * COLS * (turns + 1), 2 * turns * COLS * bins_dev * 2),
        name="gram_first",
    )(curve, jnp.asarray(order, bf16), last, *firsts)
    part_a, lhs = lax.optimization_barrier((exchange(part_a, BINS[1]), lhs))
    part_b = pl.pallas_call(
        gram_last,
        out_shape=jax.ShapeDtypeStruct((n1, width // n1, turns * COLS), bf16),
        in_specs=[VMEM] * (1 + turns),
        out_specs=VMEM,
        compiler_params=PARAMS,
        cost_estimate=cost(2 * bins_dev * width * COLS * turns, turns * COLS * bins_dev * 2),
        name="gram_last",
    )(lhs, *lasts)
    part_b = exchange(part_b, BINS[1])
    packed = -(-lines * turns * width // 128 // 16) * 16
    across = pl.pallas_call(
        functools.partial(add_across, turns),
        out_shape=jax.ShapeDtypeStruct((n0, packed, 128), bf16),
        in_specs=[VMEM] * 2,
        out_specs=VMEM,
        scratch_shapes=[pltpu.VMEM((n0, packed, 128), f32)],
        compiler_params=PARAMS,
        name="add_across",
    )(part_a, part_b)
    return pl.pallas_call(
        functools.partial(add_along, 1.0 / (bins_dev * owners)),
        out_shape=jax.ShapeDtypeStruct((lines, turns * width), f32),
        in_specs=[VMEM],
        out_specs=VMEM,
        compiler_params=PARAMS,
        name="add_along",
    )(exchange(across, BINS[0]))


def solution(mesh):
    split = Mesh(mesh.devices.reshape(16, 4, mesh.shape["params"]), ("bins_0", "bins_1", "params"))
    placed = (P(BINS), P(BINS, "params"), P(BINS), P(BINS), P(BINS))
    return jax.shard_map(
        body, mesh=split, in_specs=placed, out_specs=P(PARAMS_BINS, None), check_vma=False
    )
```

```python
import functools

import jax
import jax.numpy as jnp
import numpy as np
from jax import lax
from jax.experimental import pallas as pl
from jax.experimental.pallas import tpu as pltpu
from jax.sharding import Mesh
from jax.sharding import PartitionSpec as P

BINS = ("bins_0", "bins_1")
PARAMS_BINS = ("params", "bins_0", "bins_1")
CAP = 72
EXTRA = 8
WIN = 96
COLS = 128
KB = 512
VMEM = pl.BlockSpec(memory_space=pltpu.VMEM)
SMEM = pl.BlockSpec(memory_space=pltpu.SMEM)
PARAMS = pltpu.CompilerParams(vmem_limit_bytes=24 * 2**20)


def cost(flops, moved):
    return pl.CostEstimate(flops=flops, bytes_accessed=moved, transcendentals=0)


def pick_rows(start, w_ref, events, cols):
    base = jnp.minimum((start // 16) * 16, events - WIN)
    base = pl.multiple_of(base, 16)
    off = start - base
    row = lax.broadcasted_iota(jnp.int32, (CAP, WIN), 0)
    col = lax.broadcasted_iota(jnp.int32, (CAP, WIN), 1)
    choose = jnp.where(col == row + off, 1.0, 0.0).astype(jnp.bfloat16)
    window = w_ref[pl.ds(base, WIN), cols]
    return jnp.dot(choose, window, preferred_element_type=jnp.float32)


def lanes_from(ref, start):
    line = start // 128
    after = jnp.minimum(line + 1, ref.shape[0] - 1)
    off = start - line * 128
    back = lax.rem(128 - off, 128)
    lane = lax.broadcasted_iota(jnp.int32, (1, 128), 1)
    here = pltpu.roll(ref[pl.ds(line, 1), :], back, 1)
    there = pltpu.roll(ref[pl.ds(after, 1), :], back, 1)
    return jnp.where(lane < 128 - off, here, there)


def pack_first(owners, bins_dev, starts_ref, bins_ref, nominal_ref, w_ref, out_ref):
    events = w_ref.shape[0]
    lines = lax.broadcasted_iota(jnp.int32, (EXTRA, 128), 0)

    def one(o, _):
        start = starts_ref[o]
        rows = pick_rows(start, w_ref, events, slice(0, 2 * COLS))
        local = lanes_from(bins_ref, start) - o * bins_dev
        inside = (local >= 0) & (local < bins_dev)
        high = jnp.where(inside, local >> 5, -1).astype(jnp.float32)
        low = jnp.where(inside, local & 31, 0).astype(jnp.float32)
        nominal = jnp.where(inside, lanes_from(nominal_ref, start), 0.0)
        extra = jnp.where(lines == 0, high, jnp.where(lines == 1, low, jnp.where(lines == 2, nominal, 0.0)))
        out_ref[o] = jnp.concatenate([rows[:, :COLS], rows[:, COLS:], extra], axis=0).astype(jnp.bfloat16)
        return 0

    lax.fori_loop(0, owners, one, 0, unroll=8)


def pack_rest(n0, n1, place_ref, starts_ref, w_ref, *out_refs):
    events = w_ref.shape[0]

    def one(z, _):
        for turn, out_ref in enumerate(out_refs):
            start = starts_ref[z * n1 + lax.rem(place_ref[0] + turn, n1)]
            out_ref[z] = pick_rows(start, w_ref, events, slice(2 * COLS, 3 * COLS)).astype(jnp.bfloat16)
        return 0

    lax.fori_loop(0, n0, one, 0, unroll=2)


def one_hot_of(bins_ref, at, size, bins_dev):
    ids = lax.broadcasted_iota(jnp.int32, (bins_dev, size), 0)
    return jnp.where(ids == bins_ref[:, pl.ds(at, size)], 1.0, 0.0).astype(jnp.bfloat16)


def hist_first(bins_ref, nominal_ref, background_ref, observed_ref, left_ref, right_ref, out_ref, curve_ref, acc, acc_n):
    bins_dev = out_ref.shape[0]
    acc[...] = jnp.zeros_like(acc)
    acc_n[...] = jnp.zeros_like(acc_n)

    def one(i, _):
        at = pl.multiple_of(i * KB, KB)
        hot = one_hot_of(bins_ref, at, KB, bins_dev)
        rows = jnp.concatenate([left_ref[pl.ds(at, KB), :], right_ref[pl.ds(at, KB), :]], axis=1)
        acc[...] += jnp.dot(hot, rows, preferred_element_type=jnp.float32)
        acc_n[...] += lax.dot_general(
            hot, nominal_ref[:, pl.ds(at, KB)], (((1,), (1,)), ((), ())), preferred_element_type=jnp.float32
        )
        return 0

    lax.fori_loop(0, left_ref.shape[0] // KB, one, 0)
    out_ref[...] = acc[...].astype(jnp.bfloat16)
    yields = background_ref[...] + acc_n[:, 0:1]
    curve_ref[...] = observed_ref[...] / (yields * yields)


def hist_next(bins_ref, rows_ref, out_ref, acc):
    bins_dev = out_ref.shape[0]
    acc[...] = jnp.zeros_like(acc)

    def one(i, _):
        at = pl.multiple_of(i * KB, KB)
        hot = one_hot_of(bins_ref, at, KB, bins_dev)
        acc[...] += jnp.dot(hot, rows_ref[pl.ds(at, KB), :], preferred_element_type=jnp.float32)
        return 0

    lax.fori_loop(0, rows_ref.shape[0] // KB, one, 0)
    out_ref[...] = acc[...].astype(jnp.bfloat16)


def left_side(curve_ref, order_ref, first_ref, last_ref):
    own = jnp.concatenate([first_ref[...], last_ref[...]], axis=1)
    weighted = (curve_ref[...] * own.astype(jnp.float32)).astype(jnp.bfloat16)
    return lax.dot_general(
        order_ref[...], weighted, (((1,), (1,)), ((), ())), preferred_element_type=jnp.float32
    ).astype(jnp.bfloat16)


def gram_first(slots_ref, curve_ref, order_ref, last_ref, *refs):
    firsts, (out_ref, lhs_ref) = refs[:-2], refs[-2:]
    lhs = left_side(curve_ref, order_ref, firsts[0], last_ref)
    lhs_ref[...] = lhs
    wide, step = firsts[0].shape[1], out_ref.shape[1]
    for k, part in enumerate(firsts):
        full = jnp.dot(lhs, part[...], preferred_element_type=jnp.float32).astype(jnp.bfloat16)
        at = pl.multiple_of(slots_ref[k] * wide, wide)
        for y in range(out_ref.shape[0]):
            out_ref[y, :, pl.ds(at, wide)] = full[y * step : (y + 1) * step]


def gram_last(slots_ref, lhs_ref, *refs):
    lasts, out_ref = refs[:-1], refs[-1]
    lhs = lhs_ref[...]
    wide, step = lasts[0].shape[1], out_ref.shape[1]
    for k, part in enumerate(lasts):
        full = jnp.dot(lhs, part[...], preferred_element_type=jnp.float32).astype(jnp.bfloat16)
        at = pl.multiple_of(slots_ref[k] * wide, wide)
        for y in range(out_ref.shape[0]):
            out_ref[y, :, pl.ds(at, wide)] = full[y * step : (y + 1) * step]


def add_across(turns, first_ref, last_ref, out_ref, wide):
    n0 = out_ref.shape[0]
    lines = first_ref.shape[1] // n0
    first = jnp.sum(first_ref[...].astype(jnp.float32), axis=0)
    last = jnp.sum(last_ref[...].astype(jnp.float32), axis=0)
    wide[...] = jnp.zeros_like(wide)
    for k in range(turns):
        for t in range(3):
            tile, at = (last, k * COLS) if t == 2 else (first, (2 * k + t) * COLS)
            tile = tile[:, at : at + COLS]
            at = (3 * k + t) * lines
            for z in range(n0):
                wide[z, at : at + lines] = tile[z * lines : (z + 1) * lines]
    out_ref[...] = wide[...].astype(jnp.bfloat16)


def add_along(scale, got_ref, out_ref):
    lines = out_ref.shape[0]
    total = jnp.sum(got_ref[...].astype(jnp.float32), axis=0) * scale
    for j in range(out_ref.shape[1] // 128):
        out_ref[:, j * 128 : (j + 1) * 128] = total[j * lines : (j + 1) * lines]


def from_behind(value, axis, steps):
    count = lax.axis_size(axis)
    pairs = [(source, (source + steps) % count) for source in range(count)]
    return lax.ppermute(value, axis, pairs)


def partners(tile):
    count = lax.axis_size("params")
    if count != 8:
        return [from_behind(tile, "params", -k) for k in range(1, count // 2 + 1)], list(range(1, count // 2 + 1))
    pairs = [(source, source ^ 1) for source in range(count)]
    core = lax.rem(lax.axis_index("params"), 2)
    four = from_behind(tile, "params", -4)
    two = from_behind(tile, "params", -2)
    two_other = lax.ppermute(two, "params", pairs)
    other = lax.ppermute(jnp.where(core == 1, tile, four), "params", pairs)
    return [two, four, two_other, other], [2, 4, 3 - 2 * core, 1 + 2 * core]


def exchange(value, axis):
    return lax.all_to_all(value, axis, split_axis=0, concat_axis=0, tiled=True)


def body(event_bins, event_weights, nominal, background, observed):
    bf16, f32 = jnp.bfloat16, jnp.float32
    n0, n1 = (lax.axis_size(a) for a in BINS)
    owners = n0 * n1
    groups = lax.axis_size("params")
    events, width = event_weights.shape
    bins_dev = background.shape[0]
    targets = jnp.arange(owners, dtype=jnp.int32)
    starts = jnp.sum((event_bins[None, :] < targets[:, None] * bins_dev).astype(jnp.int32), axis=1)
    place = lax.axis_index(BINS[1])
    slab = 2 * CAP + EXTRA
    send_a = pl.pallas_call(
        functools.partial(pack_first, owners, bins_dev),
        out_shape=jax.ShapeDtypeStruct((owners, slab, COLS), bf16),
        in_specs=[SMEM, VMEM, VMEM, VMEM],
        out_specs=VMEM,
        compiler_params=PARAMS,
        cost_estimate=cost(4 * owners * CAP * WIN * COLS, 2 * owners * slab * COLS * 2),
        name="pack_first",
    )(starts, event_bins.reshape(-1, 128), nominal.astype(f32).reshape(-1, 128), event_weights)
    got_a = exchange(send_a, BINS)
    sends = pl.pallas_call(
        functools.partial(pack_rest, n0, n1),
        out_shape=[jax.ShapeDtypeStruct((n0, CAP, COLS), bf16)] * n1,
        in_specs=[SMEM, SMEM, VMEM],
        out_specs=[VMEM] * n1,
        compiler_params=PARAMS,
        cost_estimate=cost(2 * owners * CAP * WIN * COLS, 2 * owners * CAP * COLS * 2),
        name="pack_rest",
    )(place.reshape(1).astype(jnp.int32), starts, event_weights)
    mid = jnp.stack([from_behind(x, BINS[1], t) if t else x for t, x in enumerate(sends)], axis=1)
    mid, got_a = lax.optimization_barrier((mid, got_a))
    got_b = exchange(mid, BINS[0])

    total = owners * CAP
    extra = got_a[:, 2 * CAP :, :CAP].astype(f32)
    local = (extra[:, 0] * 32.0 + extra[:, 1]).astype(jnp.int32)
    back = local.reshape(n0, n1, CAP)[:, ::-1]
    local_b = lax.dynamic_slice_in_dim(jnp.concatenate([back, back], axis=1), n1 - 1 - place, n1, axis=1)
    local_b = local_b.reshape(1, total)
    local = local.reshape(1, total)
    nom = jnp.broadcast_to(extra[:, 2].astype(bf16).reshape(1, total), (8, total))
    left, right = (got_a[:, i * CAP : (i + 1) * CAP].reshape(total, COLS) for i in range(2))
    first, curve = pl.pallas_call(
        hist_first,
        out_shape=[jax.ShapeDtypeStruct((bins_dev, 2 * COLS), bf16), jax.ShapeDtypeStruct((bins_dev, 1), f32)],
        in_specs=[VMEM] * 6,
        out_specs=[VMEM] * 2,
        scratch_shapes=[pltpu.VMEM((bins_dev, 2 * COLS), f32), pltpu.VMEM((bins_dev, 8), f32)],
        compiler_params=PARAMS,
        cost_estimate=cost(2 * total * bins_dev * 512, 2 * total * COLS * 2),
        name="hist_first",
    )(local, nom, background.reshape(bins_dev, 1), observed.reshape(bins_dev, 1), left, right)
    last = pl.pallas_call(
        hist_next,
        out_shape=jax.ShapeDtypeStruct((bins_dev, COLS), bf16),
        in_specs=[VMEM] * 2,
        out_specs=VMEM,
        scratch_shapes=[pltpu.VMEM((bins_dev, COLS), f32)],
        compiler_params=PARAMS,
        cost_estimate=cost(2 * total * bins_dev * 256, total * COLS * 2),
        name="hist_next",
    )(local_b, got_b.reshape(total, COLS))
    turns = groups // 2 + 1
    firsts, slots = partners(first)
    firsts = [first] + firsts
    lasts = [last] + partners(last)[0]
    slots = jnp.stack([jnp.asarray(k, jnp.int32) for k in [0] + slots])

    lines = width // owners
    j = np.arange(width)
    source = ((j % (width // n1)) // lines * n1 + j // (width // n1)) * lines + j % lines
    order = np.zeros((width, width), np.float32)
    order[j, source] = 1.0
    part_a, lhs = pl.pallas_call(
        gram_first,
        out_shape=[
            jax.ShapeDtypeStruct((n1, width // n1, turns * 2 * COLS), bf16),
            jax.ShapeDtypeStruct((width, bins_dev), bf16),
        ],
        in_specs=[SMEM] + [VMEM] * (3 + turns),
        out_specs=[VMEM] * 2,
        compiler_params=PARAMS,
        cost_estimate=cost(2 * bins_dev * width * 2 * COLS * (turns + 1), 2 * turns * COLS * bins_dev * 2),
        name="gram_first",
    )(slots, curve, jnp.asarray(order, bf16), last, *firsts)
    part_a, lhs = lax.optimization_barrier((exchange(part_a, BINS[1]), lhs))
    part_b = pl.pallas_call(
        gram_last,
        out_shape=jax.ShapeDtypeStruct((n1, width // n1, turns * COLS), bf16),
        in_specs=[SMEM] + [VMEM] * (1 + turns),
        out_specs=VMEM,
        compiler_params=PARAMS,
        cost_estimate=cost(2 * bins_dev * width * COLS * turns, turns * COLS * bins_dev * 2),
        name="gram_last",
    )(slots, lhs, *lasts)
    part_b = exchange(part_b, BINS[1])
    packed = -(-lines * turns * width // 128 // 16) * 16
    across = pl.pallas_call(
        functools.partial(add_across, turns),
        out_shape=jax.ShapeDtypeStruct((n0, packed, 128), bf16),
        in_specs=[VMEM] * 2,
        out_specs=VMEM,
        scratch_shapes=[pltpu.VMEM((n0, packed, 128), f32)],
        compiler_params=PARAMS,
        name="add_across",
    )(part_a, part_b)
    return pl.pallas_call(
        functools.partial(add_along, 1.0 / (bins_dev * owners)),
        out_shape=jax.ShapeDtypeStruct((lines, turns * width), f32),
        in_specs=[VMEM],
        out_specs=VMEM,
        compiler_params=PARAMS,
        name="add_along",
    )(exchange(across, BINS[0]))


def solution(mesh):
    split = Mesh(mesh.devices.reshape(16, 4, mesh.shape["params"]), ("bins_0", "bins_1", "params"))
    placed = (P(BINS), P(BINS, "params"), P(BINS), P(BINS), P(BINS))
    return jax.shard_map(
        body, mesh=split, in_specs=placed, out_specs=P(PARAMS_BINS, None), check_vma=False
    )
```

```python
import functools

import jax
import jax.numpy as jnp
import numpy as np
from jax import lax
from jax.experimental import pallas as pl
from jax.experimental.pallas import tpu as pltpu
from jax.sharding import Mesh
from jax.sharding import PartitionSpec as P

BINS = ("bins_0", "bins_1")
PARAMS_BINS = ("params", "bins_0", "bins_1")
CAP = 72
EXTRA = 8
WIN = 96
COLS = 128
KB = 512
VMEM = pl.BlockSpec(memory_space=pltpu.VMEM)
SMEM = pl.BlockSpec(memory_space=pltpu.SMEM)
PARAMS = pltpu.CompilerParams(vmem_limit_bytes=24 * 2**20)


def cost(flops, moved):
    return pl.CostEstimate(flops=flops, bytes_accessed=moved, transcendentals=0)


def pick_rows(start, w_ref, events, cols):
    base = jnp.minimum((start // 16) * 16, events - WIN)
    base = pl.multiple_of(base, 16)
    off = start - base
    row = lax.broadcasted_iota(jnp.int32, (CAP, WIN), 0)
    col = lax.broadcasted_iota(jnp.int32, (CAP, WIN), 1)
    choose = jnp.where(col == row + off, 1.0, 0.0).astype(jnp.bfloat16)
    window = w_ref[pl.ds(base, WIN), cols]
    return jnp.dot(choose, window, preferred_element_type=jnp.float32)


def lanes_from(ref, start):
    line = start // 128
    after = jnp.minimum(line + 1, ref.shape[0] - 1)
    off = start - line * 128
    back = lax.rem(128 - off, 128)
    lane = lax.broadcasted_iota(jnp.int32, (1, 128), 1)
    here = pltpu.roll(ref[pl.ds(line, 1), :], back, 1)
    there = pltpu.roll(ref[pl.ds(after, 1), :], back, 1)
    return jnp.where(lane < 128 - off, here, there)


def pack_first(owners, bins_dev, starts_ref, bins_ref, nominal_ref, w_ref, out_ref):
    events = w_ref.shape[0]
    lines = lax.broadcasted_iota(jnp.int32, (EXTRA, 128), 0)

    def one(o, _):
        start = starts_ref[o]
        rows = pick_rows(start, w_ref, events, slice(0, 2 * COLS))
        local = lanes_from(bins_ref, start) - o * bins_dev
        inside = (local >= 0) & (local < bins_dev)
        high = jnp.where(inside, local >> 5, -1).astype(jnp.float32)
        low = jnp.where(inside, local & 31, 0).astype(jnp.float32)
        nominal = jnp.where(inside, lanes_from(nominal_ref, start), 0.0)
        extra = jnp.where(lines == 0, high, jnp.where(lines == 1, low, jnp.where(lines == 2, nominal, 0.0)))
        out_ref[o] = jnp.concatenate([rows[:, :COLS], rows[:, COLS:], extra], axis=0).astype(jnp.bfloat16)
        return 0

    lax.fori_loop(0, owners, one, 0, unroll=8)


def pack_rest(n0, n1, place_ref, starts_ref, w_ref, *out_refs):
    events = w_ref.shape[0]

    def one(z, _):
        for turn, out_ref in enumerate(out_refs):
            start = starts_ref[z * n1 + lax.rem(place_ref[0] + turn, n1)]
            out_ref[z] = pick_rows(start, w_ref, events, slice(2 * COLS, 3 * COLS)).astype(jnp.bfloat16)
        return 0

    lax.fori_loop(0, n0, one, 0, unroll=2)


def one_hot_of(bins_ref, at, size, bins_dev):
    ids = lax.broadcasted_iota(jnp.int32, (bins_dev, size), 0)
    return jnp.where(ids == bins_ref[:, pl.ds(at, size)], 1.0, 0.0).astype(jnp.bfloat16)


def hist_first(bins_ref, nominal_ref, background_ref, observed_ref, left_ref, right_ref, out_ref, curve_ref, acc, acc_n):
    bins_dev = out_ref.shape[0]
    acc[...] = jnp.zeros_like(acc)
    acc_n[...] = jnp.zeros_like(acc_n)

    def one(i, _):
        at = pl.multiple_of(i * KB, KB)
        hot = one_hot_of(bins_ref, at, KB, bins_dev)
        rows = jnp.concatenate([left_ref[pl.ds(at, KB), :], right_ref[pl.ds(at, KB), :]], axis=1)
        acc[...] += jnp.dot(hot, rows, preferred_element_type=jnp.float32)
        acc_n[...] += lax.dot_general(
            hot, nominal_ref[:, pl.ds(at, KB)], (((1,), (1,)), ((), ())), preferred_element_type=jnp.float32
        )
        return 0

    lax.fori_loop(0, left_ref.shape[0] // KB, one, 0)
    out_ref[...] = acc[...].astype(jnp.bfloat16)
    yields = background_ref[...] + acc_n[:, 0:1]
    curve_ref[...] = observed_ref[...] / (yields * yields)


def hist_next(bins_ref, rows_ref, out_ref, acc):
    bins_dev = out_ref.shape[0]
    acc[...] = jnp.zeros_like(acc)

    def one(i, _):
        at = pl.multiple_of(i * KB, KB)
        hot = one_hot_of(bins_ref, at, KB, bins_dev)
        acc[...] += jnp.dot(hot, rows_ref[pl.ds(at, KB), :], preferred_element_type=jnp.float32)
        return 0

    lax.fori_loop(0, rows_ref.shape[0] // KB, one, 0)
    out_ref[...] = acc[...].astype(jnp.bfloat16)


def left_side(curve_ref, order_ref, first_ref, last_ref):
    own = jnp.concatenate([first_ref[...], last_ref[...]], axis=1)
    weighted = (curve_ref[...] * own.astype(jnp.float32)).astype(jnp.bfloat16)
    return lax.dot_general(
        order_ref[...], weighted, (((1,), (1,)), ((), ())), preferred_element_type=jnp.float32
    ).astype(jnp.bfloat16)


def gram_first(slots_ref, curve_ref, order_ref, last_ref, *refs):
    firsts, (out_ref, lhs_ref) = refs[:-2], refs[-2:]
    lhs = left_side(curve_ref, order_ref, firsts[0], last_ref)
    lhs_ref[...] = lhs
    wide, step = firsts[0].shape[1], out_ref.shape[1]
    for k, part in enumerate(firsts):
        full = jnp.dot(lhs, part[...], preferred_element_type=jnp.float32).astype(jnp.bfloat16)
        at = pl.multiple_of(slots_ref[k] * wide, wide)
        for y in range(out_ref.shape[0]):
            out_ref[y, :, pl.ds(at, wide)] = full[y * step : (y + 1) * step]


def gram_last(n1, slots_ref, place_ref, lhs_ref, *refs):
    lasts, out_refs = refs[:-n1], refs[-n1:]
    step = out_refs[0].shape[0]
    wide = lasts[0].shape[1]
    for turn, out_ref in enumerate(out_refs):
        at = pl.multiple_of(lax.rem(place_ref[0] + turn, n1) * step, step)
        lhs = lhs_ref[pl.ds(at, step), :]
        for k, part in enumerate(lasts):
            full = jnp.dot(lhs, part[...], preferred_element_type=jnp.float32).astype(jnp.bfloat16)
            out_ref[:, pl.ds(pl.multiple_of(slots_ref[k] * wide, wide), wide)] = full


def rows_by_z(total, out_ref, wide):
    n0 = out_ref.shape[0]
    lines = total.shape[0] // n0
    wide[...] = jnp.zeros_like(wide)
    for j in range(total.shape[1] // COLS):
        for z in range(n0):
            wide[z, j * lines : (j + 1) * lines] = total[z * lines : (z + 1) * lines, j * COLS : (j + 1) * COLS]
    out_ref[...] = wide[...].astype(jnp.bfloat16)


def add_first(got_ref, out_ref, wide):
    rows_by_z(jnp.sum(got_ref[...].astype(jnp.float32), axis=0), out_ref, wide)


def add_last(*refs):
    total = refs[0][...].astype(jnp.float32)
    for ref in refs[1:-2]:
        total += ref[...].astype(jnp.float32)
    rows_by_z(total, *refs[-2:])


def add_along(scale, turns, first_ref, last_ref, out_ref):
    lines = out_ref.shape[0]
    first = jnp.sum(first_ref[...].astype(jnp.float32), axis=0) * scale
    last = jnp.sum(last_ref[...].astype(jnp.float32), axis=0) * scale
    for k in range(turns):
        for t in range(3):
            tile, j = (last, k) if t == 2 else (first, 2 * k + t)
            at = (3 * k + t) * COLS
            out_ref[:, at : at + COLS] = tile[j * lines : (j + 1) * lines]


def from_behind(value, axis, steps):
    count = lax.axis_size(axis)
    pairs = [(source, (source + steps) % count) for source in range(count)]
    return lax.ppermute(value, axis, pairs)


def partners(tile):
    count = lax.axis_size("params")
    if count != 8:
        return [from_behind(tile, "params", -k) for k in range(1, count // 2 + 1)], list(range(1, count // 2 + 1))
    pairs = [(source, source ^ 1) for source in range(count)]
    core = lax.rem(lax.axis_index("params"), 2)
    four = from_behind(tile, "params", -4)
    two = from_behind(tile, "params", -2)
    two_other = lax.ppermute(two, "params", pairs)
    other = lax.ppermute(jnp.where(core == 1, tile, four), "params", pairs)
    return [two, four, two_other, other], [2, 4, 3 - 2 * core, 1 + 2 * core]


def exchange(value, axis):
    return lax.all_to_all(value, axis, split_axis=0, concat_axis=0, tiled=True)


def body(event_bins, event_weights, nominal, background, observed):
    bf16, f32 = jnp.bfloat16, jnp.float32
    n0, n1 = (lax.axis_size(a) for a in BINS)
    owners = n0 * n1
    groups = lax.axis_size("params")
    events, width = event_weights.shape
    bins_dev = background.shape[0]
    targets = jnp.arange(owners, dtype=jnp.int32)
    starts = jnp.sum((event_bins[None, :] < targets[:, None] * bins_dev).astype(jnp.int32), axis=1)
    place = lax.axis_index(BINS[1])
    slab = 2 * CAP + EXTRA
    send_a = pl.pallas_call(
        functools.partial(pack_first, owners, bins_dev),
        out_shape=jax.ShapeDtypeStruct((owners, slab, COLS), bf16),
        in_specs=[SMEM, VMEM, VMEM, VMEM],
        out_specs=VMEM,
        compiler_params=PARAMS,
        cost_estimate=cost(4 * owners * CAP * WIN * COLS, 2 * owners * slab * COLS * 2),
        name="pack_first",
    )(starts, event_bins.reshape(-1, 128), nominal.astype(f32).reshape(-1, 128), event_weights)
    got_a = exchange(send_a, BINS)
    sends = pl.pallas_call(
        functools.partial(pack_rest, n0, n1),
        out_shape=[jax.ShapeDtypeStruct((n0, CAP, COLS), bf16)] * n1,
        in_specs=[SMEM, SMEM, VMEM],
        out_specs=[VMEM] * n1,
        compiler_params=PARAMS,
        cost_estimate=cost(2 * owners * CAP * WIN * COLS, 2 * owners * CAP * COLS * 2),
        name="pack_rest",
    )(place.reshape(1).astype(jnp.int32), starts, event_weights)
    mid = jnp.stack([from_behind(x, BINS[1], t) if t else x for t, x in enumerate(sends)], axis=1)
    got_b = exchange(mid, BINS[0])

    total = owners * CAP
    extra = got_a[:, 2 * CAP :, :CAP].astype(f32)
    local = (extra[:, 0] * 32.0 + extra[:, 1]).astype(jnp.int32)
    back = local.reshape(n0, n1, CAP)[:, ::-1]
    local_b = lax.dynamic_slice_in_dim(jnp.concatenate([back, back], axis=1), n1 - 1 - place, n1, axis=1)
    local_b = local_b.reshape(1, total)
    local = local.reshape(1, total)
    nom = jnp.broadcast_to(extra[:, 2].astype(bf16).reshape(1, total), (8, total))
    left, right = (got_a[:, i * CAP : (i + 1) * CAP].reshape(total, COLS) for i in range(2))
    first, curve = pl.pallas_call(
        hist_first,
        out_shape=[jax.ShapeDtypeStruct((bins_dev, 2 * COLS), bf16), jax.ShapeDtypeStruct((bins_dev, 1), f32)],
        in_specs=[VMEM] * 6,
        out_specs=[VMEM] * 2,
        scratch_shapes=[pltpu.VMEM((bins_dev, 2 * COLS), f32), pltpu.VMEM((bins_dev, 8), f32)],
        compiler_params=PARAMS,
        cost_estimate=cost(2 * total * bins_dev * 512, 2 * total * COLS * 2),
        name="hist_first",
    )(local, nom, background.reshape(bins_dev, 1), observed.reshape(bins_dev, 1), left, right)
    last = pl.pallas_call(
        hist_next,
        out_shape=jax.ShapeDtypeStruct((bins_dev, COLS), bf16),
        in_specs=[VMEM] * 2,
        out_specs=VMEM,
        scratch_shapes=[pltpu.VMEM((bins_dev, COLS), f32)],
        compiler_params=PARAMS,
        cost_estimate=cost(2 * total * bins_dev * 256, total * COLS * 2),
        name="hist_next",
    )(local_b, got_b.reshape(total, COLS))
    turns = groups // 2 + 1
    firsts, slots = partners(first)
    firsts = [first] + firsts
    lasts = [last] + partners(last)[0]
    slots = jnp.stack([jnp.asarray(k, jnp.int32) for k in [0] + slots])

    lines = width // owners
    j = np.arange(width)
    source = ((j % (width // n1)) // lines * n1 + j // (width // n1)) * lines + j % lines
    order = np.zeros((width, width), np.float32)
    order[j, source] = 1.0
    part_a, lhs = pl.pallas_call(
        gram_first,
        out_shape=[
            jax.ShapeDtypeStruct((n1, width // n1, turns * 2 * COLS), bf16),
            jax.ShapeDtypeStruct((width, bins_dev), bf16),
        ],
        in_specs=[SMEM] + [VMEM] * (3 + turns),
        out_specs=[VMEM] * 2,
        compiler_params=PARAMS,
        cost_estimate=cost(2 * bins_dev * width * 2 * COLS * (turns + 1), 2 * turns * COLS * bins_dev * 2),
        name="gram_first",
    )(slots, curve, jnp.asarray(order, bf16), last, *firsts)
    part_a = lax.optimization_barrier((exchange(part_a, BINS[1]), *lasts[1:]))[0]
    parts_b = pl.pallas_call(
        functools.partial(gram_last, n1),
        out_shape=[jax.ShapeDtypeStruct((width // n1, turns * COLS), bf16)] * n1,
        in_specs=[SMEM, SMEM] + [VMEM] * (1 + turns),
        out_specs=[VMEM] * n1,
        compiler_params=PARAMS,
        cost_estimate=cost(2 * bins_dev * width * COLS * turns, turns * COLS * bins_dev * 2),
        name="gram_last",
    )(slots, place.reshape(1).astype(jnp.int32), lhs, *lasts)
    parts_b = [from_behind(x, BINS[1], t) if t else x for t, x in enumerate(parts_b)]

    def by_z(kernel, tiles, *args):
        packed = -(-lines * tiles // 16) * 16
        return pl.pallas_call(
            kernel,
            out_shape=jax.ShapeDtypeStruct((n0, packed, COLS), bf16),
            in_specs=[VMEM] * len(args),
            out_specs=VMEM,
            scratch_shapes=[pltpu.VMEM((n0, packed, COLS), f32)],
            compiler_params=PARAMS,
            cost_estimate=cost(0, 8 * n0 * packed * COLS),
            name=kernel.__name__,
        )(*args)

    sum_a = exchange(by_z(add_first, 2 * turns, part_a), BINS[0])
    sum_b = by_z(add_last, turns, *parts_b)
    sum_b, sum_a = lax.optimization_barrier((sum_b, sum_a))
    sum_b = exchange(sum_b, BINS[0])
    return pl.pallas_call(
        functools.partial(add_along, 1.0 / (bins_dev * owners), turns),
        out_shape=jax.ShapeDtypeStruct((lines, turns * width), f32),
        in_specs=[VMEM] * 2,
        out_specs=VMEM,
        compiler_params=PARAMS,
        name="add_along",
    )(sum_a, sum_b)


def solution(mesh):
    split = Mesh(mesh.devices.reshape(16, 4, mesh.shape["params"]), ("bins_0", "bins_1", "params"))
    placed = (P(BINS), P(BINS, "params"), P(BINS), P(BINS), P(BINS))
    return jax.shard_map(
        body, mesh=split, in_specs=placed, out_specs=P(PARAMS_BINS, None), check_vma=False
    )
```

```python
import functools

import jax
import jax.numpy as jnp
import numpy as np
from jax import lax
from jax.experimental import pallas as pl
from jax.experimental.pallas import tpu as pltpu
from jax.sharding import Mesh
from jax.sharding import PartitionSpec as P

BINS = ("bins_0", "bins_1")
PARAMS_BINS = ("params", "bins_0", "bins_1")
CAP = 72
EXTRA = 8
WIN = 96
COLS = 128
KB = 512
VMEM = pl.BlockSpec(memory_space=pltpu.VMEM)
SMEM = pl.BlockSpec(memory_space=pltpu.SMEM)
PARAMS = pltpu.CompilerParams(vmem_limit_bytes=24 * 2**20)


def cost(flops, moved):
    return pl.CostEstimate(flops=flops, bytes_accessed=moved, transcendentals=0)


def pick_rows(start, w_ref, events, cols):
    base = jnp.minimum((start // 16) * 16, events - WIN)
    base = pl.multiple_of(base, 16)
    off = start - base
    row = lax.broadcasted_iota(jnp.int32, (CAP, WIN), 0)
    col = lax.broadcasted_iota(jnp.int32, (CAP, WIN), 1)
    choose = jnp.where(col == row + off, 1.0, 0.0).astype(jnp.bfloat16)
    window = w_ref[pl.ds(base, WIN), cols]
    return jnp.dot(choose, window, preferred_element_type=jnp.float32)


def lanes_from(ref, start):
    line = start // 128
    after = jnp.minimum(line + 1, ref.shape[0] - 1)
    off = start - line * 128
    back = lax.rem(128 - off, 128)
    lane = lax.broadcasted_iota(jnp.int32, (1, 128), 1)
    here = pltpu.roll(ref[pl.ds(line, 1), :], back, 1)
    there = pltpu.roll(ref[pl.ds(after, 1), :], back, 1)
    return jnp.where(lane < 128 - off, here, there)


def pack_first(owners, bins_dev, starts_ref, bins_ref, nominal_ref, w_ref, out_ref):
    events = w_ref.shape[0]
    lines = lax.broadcasted_iota(jnp.int32, (EXTRA, 128), 0)

    def one(o, _):
        start = starts_ref[o]
        rows = pick_rows(start, w_ref, events, slice(0, 2 * COLS))
        local = lanes_from(bins_ref, start) - o * bins_dev
        inside = (local >= 0) & (local < bins_dev)
        high = jnp.where(inside, local >> 5, -1).astype(jnp.float32)
        low = jnp.where(inside, local & 31, 0).astype(jnp.float32)
        nominal = jnp.where(inside, lanes_from(nominal_ref, start), 0.0)
        extra = jnp.where(lines == 0, high, jnp.where(lines == 1, low, jnp.where(lines == 2, nominal, 0.0)))
        out_ref[o] = jnp.concatenate([rows[:, :COLS], rows[:, COLS:], extra], axis=0).astype(jnp.bfloat16)
        return 0

    lax.fori_loop(0, owners, one, 0, unroll=8)


def pack_rest(n0, n1, place_ref, starts_ref, w_ref, *out_refs):
    events = w_ref.shape[0]

    def one(z, _):
        for turn, out_ref in enumerate(out_refs):
            start = starts_ref[z * n1 + lax.rem(place_ref[0] + turn, n1)]
            out_ref[z] = pick_rows(start, w_ref, events, slice(2 * COLS, 3 * COLS)).astype(jnp.bfloat16)
        return 0

    lax.fori_loop(0, n0, one, 0, unroll=2)


def one_hot_of(bins_ref, at, size, bins_dev):
    ids = lax.broadcasted_iota(jnp.int32, (bins_dev, size), 0)
    return jnp.where(ids == bins_ref[:, pl.ds(at, size)], 1.0, 0.0).astype(jnp.bfloat16)


def hist_first(bins_ref, nominal_ref, background_ref, observed_ref, left_ref, right_ref, out_ref, curve_ref, acc, acc_n):
    bins_dev = out_ref.shape[0]
    acc[...] = jnp.zeros_like(acc)
    acc_n[...] = jnp.zeros_like(acc_n)

    def one(i, _):
        at = pl.multiple_of(i * KB, KB)
        hot = one_hot_of(bins_ref, at, KB, bins_dev)
        rows = jnp.concatenate([left_ref[pl.ds(at, KB), :], right_ref[pl.ds(at, KB), :]], axis=1)
        acc[...] += jnp.dot(hot, rows, preferred_element_type=jnp.float32)
        acc_n[...] += lax.dot_general(
            hot, nominal_ref[:, pl.ds(at, KB)], (((1,), (1,)), ((), ())), preferred_element_type=jnp.float32
        )
        return 0

    lax.fori_loop(0, left_ref.shape[0] // KB, one, 0)
    out_ref[...] = acc[...].astype(jnp.bfloat16)
    yields = background_ref[...] + acc_n[:, 0:1]
    curve_ref[...] = observed_ref[...] / (yields * yields)


def hist_next(bins_ref, rows_ref, out_ref, acc):
    bins_dev = out_ref.shape[0]
    acc[...] = jnp.zeros_like(acc)

    def one(i, _):
        at = pl.multiple_of(i * KB, KB)
        hot = one_hot_of(bins_ref, at, KB, bins_dev)
        acc[...] += jnp.dot(hot, rows_ref[pl.ds(at, KB), :], preferred_element_type=jnp.float32)
        return 0

    lax.fori_loop(0, rows_ref.shape[0] // KB, one, 0)
    out_ref[...] = acc[...].astype(jnp.bfloat16)


def left_side(curve_ref, order_ref, first_ref, last_ref):
    own = jnp.concatenate([first_ref[...], last_ref[...]], axis=1)
    weighted = (curve_ref[...] * own.astype(jnp.float32)).astype(jnp.bfloat16)
    return lax.dot_general(
        order_ref[...], weighted, (((1,), (1,)), ((), ())), preferred_element_type=jnp.float32
    ).astype(jnp.bfloat16)


def gram_first(slots_ref, curve_ref, order_ref, last_ref, *refs):
    firsts, (out_ref, lhs_ref) = refs[:-2], refs[-2:]
    lhs = left_side(curve_ref, order_ref, firsts[0], last_ref)
    lhs_ref[...] = lhs
    wide, step = firsts[0].shape[1], out_ref.shape[1]
    for k, part in enumerate(firsts):
        full = jnp.dot(lhs, part[...], preferred_element_type=jnp.float32).astype(jnp.bfloat16)
        at = pl.multiple_of(slots_ref[k] * wide, wide)
        for y in range(out_ref.shape[0]):
            out_ref[y, :, pl.ds(at, wide)] = full[y * step : (y + 1) * step]


def gram_last(slots_ref, lhs_ref, *refs):
    lasts, out_ref = refs[:-1], refs[-1]
    lhs = lhs_ref[...]
    wide, step = lasts[0].shape[1], out_ref.shape[1]
    for k, part in enumerate(lasts):
        full = jnp.dot(lhs, part[...], preferred_element_type=jnp.float32).astype(jnp.bfloat16)
        at = pl.multiple_of(slots_ref[k] * wide, wide)
        for y in range(out_ref.shape[0]):
            out_ref[y, :, pl.ds(at, wide)] = full[y * step : (y + 1) * step]


def add_across(turns, first_ref, last_ref, out_ref, wide):
    n0 = out_ref.shape[0]
    lines = first_ref.shape[1] // n0
    first = jnp.sum(first_ref[...].astype(jnp.float32), axis=0)
    last = jnp.sum(last_ref[...].astype(jnp.float32), axis=0)
    wide[...] = jnp.zeros_like(wide)
    for k in range(turns):
        for t in range(3):
            tile, at = (last, k * COLS) if t == 2 else (first, (2 * k + t) * COLS)
            tile = tile[:, at : at + COLS]
            at = (3 * k + t) * lines
            for z in range(n0):
                wide[z, at : at + lines] = tile[z * lines : (z + 1) * lines]
    out_ref[...] = wide[...].astype(jnp.bfloat16)


def add_along(scale, got_ref, out_ref):
    lines = out_ref.shape[0]
    total = jnp.sum(got_ref[...].astype(jnp.float32), axis=0) * scale
    for j in range(out_ref.shape[1] // 128):
        out_ref[:, j * 128 : (j + 1) * 128] = total[j * lines : (j + 1) * lines]


def from_behind(value, axis, steps):
    count = lax.axis_size(axis)
    pairs = [(source, (source + steps) % count) for source in range(count)]
    return lax.ppermute(value, axis, pairs)


def partners(tile):
    count = lax.axis_size("params")
    if count != 8:
        return [from_behind(tile, "params", -k) for k in range(1, count // 2 + 1)], list(range(1, count // 2 + 1))
    pairs = [(source, source ^ 1) for source in range(count)]
    core = lax.rem(lax.axis_index("params"), 2)
    four = from_behind(tile, "params", -4)
    two = from_behind(tile, "params", -2)
    two_other = lax.ppermute(two, "params", pairs)
    other = lax.ppermute(jnp.where(core == 1, tile, four), "params", pairs)
    return [two, four, two_other, other], [2, 4, 3 - 2 * core, 1 + 2 * core]


def exchange(value, axis):
    return lax.all_to_all(value, axis, split_axis=0, concat_axis=0, tiled=True)


def body(event_bins, event_weights, nominal, background, observed):
    bf16, f32 = jnp.bfloat16, jnp.float32
    n0, n1 = (lax.axis_size(a) for a in BINS)
    owners = n0 * n1
    groups = lax.axis_size("params")
    events, width = event_weights.shape
    bins_dev = background.shape[0]
    targets = jnp.arange(owners, dtype=jnp.int32)
    starts = jnp.sum((event_bins[None, :] < targets[:, None] * bins_dev).astype(jnp.int32), axis=1)
    place = lax.axis_index(BINS[1])
    slab = 2 * CAP + EXTRA
    send_a = pl.pallas_call(
        functools.partial(pack_first, owners, bins_dev),
        out_shape=jax.ShapeDtypeStruct((owners, slab, COLS), bf16),
        in_specs=[SMEM, VMEM, VMEM, VMEM],
        out_specs=VMEM,
        compiler_params=PARAMS,
        cost_estimate=cost(4 * owners * CAP * WIN * COLS, 2 * owners * slab * COLS * 2),
        name="pack_first",
    )(starts, event_bins.reshape(-1, 128), nominal.astype(f32).reshape(-1, 128), event_weights)
    got_a = exchange(send_a, BINS)
    sends = pl.pallas_call(
        functools.partial(pack_rest, n0, n1),
        out_shape=[jax.ShapeDtypeStruct((n0, CAP, COLS), bf16)] * n1,
        in_specs=[SMEM, SMEM, VMEM],
        out_specs=[VMEM] * n1,
        compiler_params=PARAMS,
        cost_estimate=cost(2 * owners * CAP * WIN * COLS, 2 * owners * CAP * COLS * 2),
        name="pack_rest",
    )(place.reshape(1).astype(jnp.int32), starts, event_weights)
    mid = jnp.stack([from_behind(x, BINS[1], t) if t else x for t, x in enumerate(sends)], axis=1)
    got_b = exchange(mid, BINS[0])

    total = owners * CAP
    extra = got_a[:, 2 * CAP :, :CAP].astype(f32)
    local = (extra[:, 0] * 32.0 + extra[:, 1]).astype(jnp.int32)
    back = local.reshape(n0, n1, CAP)[:, ::-1]
    local_b = lax.dynamic_slice_in_dim(jnp.concatenate([back, back], axis=1), n1 - 1 - place, n1, axis=1)
    local_b = local_b.reshape(1, total)
    local = local.reshape(1, total)
    nom = jnp.broadcast_to(extra[:, 2].astype(bf16).reshape(1, total), (8, total))
    left, right = (got_a[:, i * CAP : (i + 1) * CAP].reshape(total, COLS) for i in range(2))
    first, curve = pl.pallas_call(
        hist_first,
        out_shape=[jax.ShapeDtypeStruct((bins_dev, 2 * COLS), bf16), jax.ShapeDtypeStruct((bins_dev, 1), f32)],
        in_specs=[VMEM] * 6,
        out_specs=[VMEM] * 2,
        scratch_shapes=[pltpu.VMEM((bins_dev, 2 * COLS), f32), pltpu.VMEM((bins_dev, 8), f32)],
        compiler_params=PARAMS,
        cost_estimate=cost(2 * total * bins_dev * 512, 2 * total * COLS * 2),
        name="hist_first",
    )(local, nom, background.reshape(bins_dev, 1), observed.reshape(bins_dev, 1), left, right)
    last = pl.pallas_call(
        hist_next,
        out_shape=jax.ShapeDtypeStruct((bins_dev, COLS), bf16),
        in_specs=[VMEM] * 2,
        out_specs=VMEM,
        scratch_shapes=[pltpu.VMEM((bins_dev, COLS), f32)],
        compiler_params=PARAMS,
        cost_estimate=cost(2 * total * bins_dev * 256, total * COLS * 2),
        name="hist_next",
    )(local_b, got_b.reshape(total, COLS))
    turns = groups // 2 + 1
    firsts, slots = partners(first)
    firsts = [first] + firsts
    lasts = [last] + partners(last)[0]
    slots = jnp.stack([jnp.asarray(k, jnp.int32) for k in [0] + slots])

    lines = width // owners
    j = np.arange(width)
    source = ((j % (width // n1)) // lines * n1 + j // (width // n1)) * lines + j % lines
    order = np.zeros((width, width), np.float32)
    order[j, source] = 1.0
    part_a, lhs = pl.pallas_call(
        gram_first,
        out_shape=[
            jax.ShapeDtypeStruct((n1, width // n1, turns * 2 * COLS), bf16),
            jax.ShapeDtypeStruct((width, bins_dev), bf16),
        ],
        in_specs=[SMEM] + [VMEM] * (3 + turns),
        out_specs=[VMEM] * 2,
        compiler_params=PARAMS,
        cost_estimate=cost(2 * bins_dev * width * 2 * COLS * (turns + 1), 2 * turns * COLS * bins_dev * 2),
        name="gram_first",
    )(slots, curve, jnp.asarray(order, bf16), last, *firsts)
    part_a, lhs = lax.optimization_barrier((exchange(part_a, BINS[1]), lhs))
    part_b = pl.pallas_call(
        gram_last,
        out_shape=jax.ShapeDtypeStruct((n1, width // n1, turns * COLS), bf16),
        in_specs=[SMEM] + [VMEM] * (1 + turns),
        out_specs=VMEM,
        compiler_params=PARAMS,
        cost_estimate=cost(2 * bins_dev * width * COLS * turns, turns * COLS * bins_dev * 2),
        name="gram_last",
    )(slots, lhs, *lasts)
    part_b = exchange(part_b, BINS[1])
    packed = -(-lines * turns * width // 128 // 16) * 16
    across = pl.pallas_call(
        functools.partial(add_across, turns),
        out_shape=jax.ShapeDtypeStruct((n0, packed, 128), bf16),
        in_specs=[VMEM] * 2,
        out_specs=VMEM,
        scratch_shapes=[pltpu.VMEM((n0, packed, 128), f32)],
        compiler_params=PARAMS,
        name="add_across",
    )(part_a, part_b)
    return pl.pallas_call(
        functools.partial(add_along, 1.0 / (bins_dev * owners)),
        out_shape=jax.ShapeDtypeStruct((lines, turns * width), f32),
        in_specs=[VMEM],
        out_specs=VMEM,
        compiler_params=PARAMS,
        name="add_along",
    )(exchange(across, BINS[0]))


def solution(mesh):
    split = Mesh(mesh.devices.reshape(16, 4, mesh.shape["params"]), ("bins_0", "bins_1", "params"))
    placed = (P(BINS), P(BINS, "params"), P(BINS), P(BINS), P(BINS))
    return jax.shard_map(
        body, mesh=split, in_specs=placed, out_specs=P(PARAMS_BINS, None), check_vma=False
    )
```

```python
import functools

import jax
import jax.numpy as jnp
import numpy as np
from jax import lax
from jax.experimental import pallas as pl
from jax.experimental.pallas import tpu as pltpu
from jax.sharding import Mesh
from jax.sharding import PartitionSpec as P

BINS = ("bins_0", "bins_1")
PARAMS_BINS = ("params", "bins_0", "bins_1")
CAP = 72
EXTRA = 8
WIN = 96
COLS = 128
KB = 512
VMEM = pl.BlockSpec(memory_space=pltpu.VMEM)
SMEM = pl.BlockSpec(memory_space=pltpu.SMEM)
PARAMS = pltpu.CompilerParams(vmem_limit_bytes=24 * 2**20)


def cost(flops, moved):
    return pl.CostEstimate(flops=flops, bytes_accessed=moved, transcendentals=0)


def pick_rows(start, w_ref, events, cols):
    base = jnp.minimum((start // 16) * 16, events - WIN)
    base = pl.multiple_of(base, 16)
    off = start - base
    row = lax.broadcasted_iota(jnp.int32, (CAP, WIN), 0)
    col = lax.broadcasted_iota(jnp.int32, (CAP, WIN), 1)
    choose = jnp.where(col == row + off, 1.0, 0.0).astype(jnp.bfloat16)
    window = w_ref[pl.ds(base, WIN), cols]
    return jnp.dot(choose, window, preferred_element_type=jnp.float32)


def lanes_from(ref, start):
    line = start // 128
    after = jnp.minimum(line + 1, ref.shape[0] - 1)
    off = start - line * 128
    back = lax.rem(128 - off, 128)
    lane = lax.broadcasted_iota(jnp.int32, (1, 128), 1)
    here = pltpu.roll(ref[pl.ds(line, 1), :], back, 1)
    there = pltpu.roll(ref[pl.ds(after, 1), :], back, 1)
    return jnp.where(lane < 128 - off, here, there)


def pack_first(owners, bins_dev, starts_ref, bins_ref, nominal_ref, w_ref, out_ref):
    events = w_ref.shape[0]
    lines = lax.broadcasted_iota(jnp.int32, (EXTRA, 128), 0)

    def one(o, _):
        start = starts_ref[o]
        rows = pick_rows(start, w_ref, events, slice(0, 2 * COLS))
        local = lanes_from(bins_ref, start) - o * bins_dev
        inside = (local >= 0) & (local < bins_dev)
        high = jnp.where(inside, local >> 5, -1).astype(jnp.float32)
        low = jnp.where(inside, local & 31, 0).astype(jnp.float32)
        nominal = jnp.where(inside, lanes_from(nominal_ref, start), 0.0)
        extra = jnp.where(lines == 0, high, jnp.where(lines == 1, low, jnp.where(lines == 2, nominal, 0.0)))
        out_ref[o] = jnp.concatenate([rows[:, :COLS], rows[:, COLS:], extra], axis=0).astype(jnp.bfloat16)
        return 0

    lax.fori_loop(0, owners, one, 0, unroll=8)


def pack_rest(n0, n1, place_ref, starts_ref, w_ref, *out_refs):
    events = w_ref.shape[0]

    def one(z, _):
        for turn, out_ref in enumerate(out_refs):
            start = starts_ref[z * n1 + lax.rem(place_ref[0] + turn, n1)]
            out_ref[z] = pick_rows(start, w_ref, events, slice(2 * COLS, 3 * COLS)).astype(jnp.bfloat16)
        return 0

    lax.fori_loop(0, n0, one, 0, unroll=2)


def one_hot_of(bins_ref, at, size, bins_dev):
    ids = lax.broadcasted_iota(jnp.int32, (bins_dev, size), 0)
    return jnp.where(ids == bins_ref[:, pl.ds(at, size)], 1.0, 0.0).astype(jnp.bfloat16)


def hist_first(bins_ref, nominal_ref, background_ref, observed_ref, left_ref, right_ref, out_ref, curve_ref, acc, acc_n):
    bins_dev = out_ref.shape[0]
    acc[...] = jnp.zeros_like(acc)
    acc_n[...] = jnp.zeros_like(acc_n)

    def one(i, _):
        at = pl.multiple_of(i * KB, KB)
        hot = one_hot_of(bins_ref, at, KB, bins_dev)
        rows = jnp.concatenate([left_ref[pl.ds(at, KB), :], right_ref[pl.ds(at, KB), :]], axis=1)
        acc[...] += jnp.dot(hot, rows, preferred_element_type=jnp.float32)
        acc_n[...] += lax.dot_general(
            hot, nominal_ref[:, pl.ds(at, KB)], (((1,), (1,)), ((), ())), preferred_element_type=jnp.float32
        )
        return 0

    lax.fori_loop(0, left_ref.shape[0] // KB, one, 0)
    out_ref[...] = acc[...].astype(jnp.bfloat16)
    yields = background_ref[...] + acc_n[:, 0:1]
    curve_ref[...] = observed_ref[...] / (yields * yields)


def hist_next(bins_ref, rows_ref, out_ref, acc):
    bins_dev = out_ref.shape[0]
    acc[...] = jnp.zeros_like(acc)

    def one(i, _):
        at = pl.multiple_of(i * KB, KB)
        hot = one_hot_of(bins_ref, at, KB, bins_dev)
        acc[...] += jnp.dot(hot, rows_ref[pl.ds(at, KB), :], preferred_element_type=jnp.float32)
        return 0

    lax.fori_loop(0, rows_ref.shape[0] // KB, one, 0)
    out_ref[...] = acc[...].astype(jnp.bfloat16)


def side_of(curve_ref, order, own_ref):
    weighted = (curve_ref[...] * own_ref[...].astype(jnp.float32)).astype(jnp.bfloat16)
    return lax.dot_general(order, weighted, (((1,), (1,)), ((), ())), preferred_element_type=jnp.float32)


def side_first(curve_ref, order_ref, first_ref, out_ref):
    out_ref[...] = side_of(curve_ref, order_ref[:, : 2 * COLS], first_ref).astype(jnp.bfloat16)


def gram_first(slots_ref, curve_ref, order_ref, side_ref, last_ref, *refs):
    firsts, (out_ref, lhs_ref) = refs[:-2], refs[-2:]
    lhs = side_ref[...] + side_of(curve_ref, order_ref[:, 2 * COLS :], last_ref).astype(jnp.bfloat16)
    lhs_ref[...] = lhs
    wide, step = firsts[0].shape[1], out_ref.shape[1]
    for k, part in enumerate(firsts):
        full = jnp.dot(lhs, part[...], preferred_element_type=jnp.float32).astype(jnp.bfloat16)
        at = pl.multiple_of(slots_ref[k] * wide, wide)
        for y in range(out_ref.shape[0]):
            out_ref[y, :, pl.ds(at, wide)] = full[y * step : (y + 1) * step]


def gram_last(slots_ref, lhs_ref, *refs):
    lasts, out_ref = refs[:-1], refs[-1]
    lhs = lhs_ref[...]
    wide, step = lasts[0].shape[1], out_ref.shape[1]
    for k, part in enumerate(lasts):
        full = jnp.dot(lhs, part[...], preferred_element_type=jnp.float32).astype(jnp.bfloat16)
        at = pl.multiple_of(slots_ref[k] * wide, wide)
        for y in range(out_ref.shape[0]):
            out_ref[y, :, pl.ds(at, wide)] = full[y * step : (y + 1) * step]


def add_across(turns, first_ref, last_ref, out_ref, wide):
    n0 = out_ref.shape[0]
    lines = first_ref.shape[1] // n0
    first = jnp.sum(first_ref[...].astype(jnp.float32), axis=0)
    last = jnp.sum(last_ref[...].astype(jnp.float32), axis=0)
    wide[...] = jnp.zeros_like(wide)
    for k in range(turns):
        for t in range(3):
            tile, at = (last, k * COLS) if t == 2 else (first, (2 * k + t) * COLS)
            tile = tile[:, at : at + COLS]
            at = (3 * k + t) * lines
            for z in range(n0):
                wide[z, at : at + lines] = tile[z * lines : (z + 1) * lines]
    out_ref[...] = wide[...].astype(jnp.bfloat16)


def add_along(scale, got_ref, out_ref):
    lines = out_ref.shape[0]
    total = jnp.sum(got_ref[...].astype(jnp.float32), axis=0) * scale
    for j in range(out_ref.shape[1] // 128):
        out_ref[:, j * 128 : (j + 1) * 128] = total[j * lines : (j + 1) * lines]


def from_behind(value, axis, steps):
    count = lax.axis_size(axis)
    pairs = [(source, (source + steps) % count) for source in range(count)]
    return lax.ppermute(value, axis, pairs)


def partners(tile):
    count = lax.axis_size("params")
    if count != 8:
        return [from_behind(tile, "params", -k) for k in range(1, count // 2 + 1)], list(range(1, count // 2 + 1))
    pairs = [(source, source ^ 1) for source in range(count)]
    core = lax.rem(lax.axis_index("params"), 2)
    four = from_behind(tile, "params", -4)
    two = from_behind(tile, "params", -2)
    two_other = lax.ppermute(two, "params", pairs)
    other = lax.ppermute(jnp.where(core == 1, tile, four), "params", pairs)
    return [two, four, two_other, other], [2, 4, 3 - 2 * core, 1 + 2 * core]


def exchange(value, axis):
    return lax.all_to_all(value, axis, split_axis=0, concat_axis=0, tiled=True)


def body(event_bins, event_weights, nominal, background, observed):
    bf16, f32 = jnp.bfloat16, jnp.float32
    n0, n1 = (lax.axis_size(a) for a in BINS)
    owners = n0 * n1
    groups = lax.axis_size("params")
    events, width = event_weights.shape
    bins_dev = background.shape[0]
    targets = jnp.arange(owners, dtype=jnp.int32)
    starts = jnp.sum((event_bins[None, :] < targets[:, None] * bins_dev).astype(jnp.int32), axis=1)
    place = lax.axis_index(BINS[1])
    slab = 2 * CAP + EXTRA
    send_a = pl.pallas_call(
        functools.partial(pack_first, owners, bins_dev),
        out_shape=jax.ShapeDtypeStruct((owners, slab, COLS), bf16),
        in_specs=[SMEM, VMEM, VMEM, VMEM],
        out_specs=VMEM,
        compiler_params=PARAMS,
        cost_estimate=cost(4 * owners * CAP * WIN * COLS, 2 * owners * slab * COLS * 2),
        name="pack_first",
    )(starts, event_bins.reshape(-1, 128), nominal.astype(f32).reshape(-1, 128), event_weights)
    got_a = exchange(send_a, BINS)
    sends = pl.pallas_call(
        functools.partial(pack_rest, n0, n1),
        out_shape=[jax.ShapeDtypeStruct((n0, CAP, COLS), bf16)] * n1,
        in_specs=[SMEM, SMEM, VMEM],
        out_specs=[VMEM] * n1,
        compiler_params=PARAMS,
        cost_estimate=cost(2 * owners * CAP * WIN * COLS, 2 * owners * CAP * COLS * 2),
        name="pack_rest",
    )(place.reshape(1).astype(jnp.int32), starts, event_weights)
    mid = jnp.stack([from_behind(x, BINS[1], t) if t else x for t, x in enumerate(sends)], axis=1)
    got_b = exchange(mid, BINS[0])

    total = owners * CAP
    extra = got_a[:, 2 * CAP :, :CAP].astype(f32)
    local = (extra[:, 0] * 32.0 + extra[:, 1]).astype(jnp.int32)
    back = local.reshape(n0, n1, CAP)[:, ::-1]
    local_b = lax.dynamic_slice_in_dim(jnp.concatenate([back, back], axis=1), n1 - 1 - place, n1, axis=1)
    local_b = local_b.reshape(1, total)
    local = local.reshape(1, total)
    nom = jnp.broadcast_to(extra[:, 2].astype(bf16).reshape(1, total), (8, total))
    left, right = (got_a[:, i * CAP : (i + 1) * CAP].reshape(total, COLS) for i in range(2))
    first, curve = pl.pallas_call(
        hist_first,
        out_shape=[jax.ShapeDtypeStruct((bins_dev, 2 * COLS), bf16), jax.ShapeDtypeStruct((bins_dev, 1), f32)],
        in_specs=[VMEM] * 6,
        out_specs=[VMEM] * 2,
        scratch_shapes=[pltpu.VMEM((bins_dev, 2 * COLS), f32), pltpu.VMEM((bins_dev, 8), f32)],
        compiler_params=PARAMS,
        cost_estimate=cost(2 * total * bins_dev * 512, 2 * total * COLS * 2),
        name="hist_first",
    )(local, nom, background.reshape(bins_dev, 1), observed.reshape(bins_dev, 1), left, right)
    lines = width // owners
    j = np.arange(width)
    source = ((j % (width // n1)) // lines * n1 + j // (width // n1)) * lines + j % lines
    order = np.zeros((width, width), np.float32)
    order[j, source] = 1.0
    side = pl.pallas_call(
        side_first,
        out_shape=jax.ShapeDtypeStruct((width, bins_dev), bf16),
        in_specs=[VMEM] * 3,
        out_specs=VMEM,
        compiler_params=PARAMS,
        cost_estimate=cost(2 * bins_dev * width * 2 * COLS, 2 * bins_dev * width * 2),
        name="side_first",
    )(curve, jnp.asarray(order, bf16), first)
    side, got_b = lax.optimization_barrier((side, got_b))
    last = pl.pallas_call(
        hist_next,
        out_shape=jax.ShapeDtypeStruct((bins_dev, COLS), bf16),
        in_specs=[VMEM] * 2,
        out_specs=VMEM,
        scratch_shapes=[pltpu.VMEM((bins_dev, COLS), f32)],
        compiler_params=PARAMS,
        cost_estimate=cost(2 * total * bins_dev * 256, total * COLS * 2),
        name="hist_next",
    )(local_b, got_b.reshape(total, COLS))
    turns = groups // 2 + 1
    firsts, slots = partners(first)
    firsts = [first] + firsts
    lasts = [last] + partners(last)[0]
    slots = jnp.stack([jnp.asarray(k, jnp.int32) for k in [0] + slots])

    part_a, lhs = pl.pallas_call(
        gram_first,
        out_shape=[
            jax.ShapeDtypeStruct((n1, width // n1, turns * 2 * COLS), bf16),
            jax.ShapeDtypeStruct((width, bins_dev), bf16),
        ],
        in_specs=[SMEM] + [VMEM] * (4 + turns),
        out_specs=[VMEM] * 2,
        compiler_params=PARAMS,
        cost_estimate=cost(2 * bins_dev * width * 2 * COLS * (turns + 1), 2 * turns * COLS * bins_dev * 2),
        name="gram_first",
    )(slots, curve, jnp.asarray(order, bf16), side, last, *firsts)
    part_a, lhs = lax.optimization_barrier((exchange(part_a, BINS[1]), lhs))
    part_b = pl.pallas_call(
        gram_last,
        out_shape=jax.ShapeDtypeStruct((n1, width // n1, turns * COLS), bf16),
        in_specs=[SMEM] + [VMEM] * (1 + turns),
        out_specs=VMEM,
        compiler_params=PARAMS,
        cost_estimate=cost(2 * bins_dev * width * COLS * turns, turns * COLS * bins_dev * 2),
        name="gram_last",
    )(slots, lhs, *lasts)
    part_b = exchange(part_b, BINS[1])
    packed = -(-lines * turns * width // 128 // 16) * 16
    across = pl.pallas_call(
        functools.partial(add_across, turns),
        out_shape=jax.ShapeDtypeStruct((n0, packed, 128), bf16),
        in_specs=[VMEM] * 2,
        out_specs=VMEM,
        scratch_shapes=[pltpu.VMEM((n0, packed, 128), f32)],
        compiler_params=PARAMS,
        name="add_across",
    )(part_a, part_b)
    return pl.pallas_call(
        functools.partial(add_along, 1.0 / (bins_dev * owners)),
        out_shape=jax.ShapeDtypeStruct((lines, turns * width), f32),
        in_specs=[VMEM],
        out_specs=VMEM,
        compiler_params=PARAMS,
        name="add_along",
    )(exchange(across, BINS[0]))


def solution(mesh):
    split = Mesh(mesh.devices.reshape(16, 4, mesh.shape["params"]), ("bins_0", "bins_1", "params"))
    placed = (P(BINS), P(BINS, "params"), P(BINS), P(BINS), P(BINS))
    return jax.shard_map(
        body, mesh=split, in_specs=placed, out_specs=P(PARAMS_BINS, None), check_vma=False
    )
```

```python
import functools

import jax
import jax.numpy as jnp
import numpy as np
from jax import lax
from jax.experimental import pallas as pl
from jax.experimental.pallas import tpu as pltpu
from jax.sharding import Mesh
from jax.sharding import PartitionSpec as P

BINS = ("bins_0", "bins_1")
PARAMS_BINS = ("params", "bins_0", "bins_1")
CAP = 72
EXTRA = 8
WIN = 96
COLS = 128
KB = 512
VMEM = pl.BlockSpec(memory_space=pltpu.VMEM)
SMEM = pl.BlockSpec(memory_space=pltpu.SMEM)
PARAMS = pltpu.CompilerParams(vmem_limit_bytes=24 * 2**20)


def cost(flops, moved):
    return pl.CostEstimate(flops=flops, bytes_accessed=moved, transcendentals=0)


def pick_rows(start, w_ref, events, cols):
    base = jnp.minimum((start // 16) * 16, events - WIN)
    base = pl.multiple_of(base, 16)
    off = start - base
    row = lax.broadcasted_iota(jnp.int32, (CAP, WIN), 0)
    col = lax.broadcasted_iota(jnp.int32, (CAP, WIN), 1)
    choose = jnp.where(col == row + off, 1.0, 0.0).astype(jnp.bfloat16)
    window = w_ref[pl.ds(base, WIN), cols]
    return jnp.dot(choose, window, preferred_element_type=jnp.float32)


def lanes_from(ref, start):
    line = start // 128
    after = jnp.minimum(line + 1, ref.shape[0] - 1)
    off = start - line * 128
    back = lax.rem(128 - off, 128)
    lane = lax.broadcasted_iota(jnp.int32, (1, 128), 1)
    here = pltpu.roll(ref[pl.ds(line, 1), :], back, 1)
    there = pltpu.roll(ref[pl.ds(after, 1), :], back, 1)
    return jnp.where(lane < 128 - off, here, there)


def pack_first(owners, bins_dev, starts_ref, bins_ref, nominal_ref, w_ref, out_ref):
    events = w_ref.shape[0]
    lines = lax.broadcasted_iota(jnp.int32, (EXTRA, 128), 0)

    def one(o, _):
        start = starts_ref[o]
        rows = pick_rows(start, w_ref, events, slice(0, 2 * COLS))
        local = lanes_from(bins_ref, start) - o * bins_dev
        inside = (local >= 0) & (local < bins_dev)
        high = jnp.where(inside, local >> 5, -1).astype(jnp.float32)
        low = jnp.where(inside, local & 31, 0).astype(jnp.float32)
        nominal = jnp.where(inside, lanes_from(nominal_ref, start), 0.0)
        extra = jnp.where(lines == 0, high, jnp.where(lines == 1, low, jnp.where(lines == 2, nominal, 0.0)))
        out_ref[o] = jnp.concatenate([rows[:, :COLS], rows[:, COLS:], extra], axis=0).astype(jnp.bfloat16)
        return 0

    lax.fori_loop(0, owners, one, 0, unroll=8)


def pack_rest(n0, n1, place_ref, starts_ref, w_ref, *out_refs):
    events = w_ref.shape[0]

    def one(z, _):
        for turn, out_ref in enumerate(out_refs):
            start = starts_ref[z * n1 + lax.rem(place_ref[0] + turn, n1)]
            out_ref[z] = pick_rows(start, w_ref, events, slice(2 * COLS, 3 * COLS)).astype(jnp.bfloat16)
        return 0

    lax.fori_loop(0, n0, one, 0, unroll=2)


def one_hot_of(bins_ref, at, size, bins_dev):
    ids = lax.broadcasted_iota(jnp.int32, (bins_dev, size), 0)
    return jnp.where(ids == bins_ref[:, pl.ds(at, size)], 1.0, 0.0).astype(jnp.bfloat16)


def hist_first(bins_ref, nominal_ref, background_ref, observed_ref, left_ref, right_ref, out_ref, curve_ref, acc, acc_n):
    bins_dev = out_ref.shape[0]
    acc[...] = jnp.zeros_like(acc)
    acc_n[...] = jnp.zeros_like(acc_n)

    def one(i, _):
        at = pl.multiple_of(i * KB, KB)
        hot = one_hot_of(bins_ref, at, KB, bins_dev)
        rows = jnp.concatenate([left_ref[pl.ds(at, KB), :], right_ref[pl.ds(at, KB), :]], axis=1)
        acc[...] += jnp.dot(hot, rows, preferred_element_type=jnp.float32)
        acc_n[...] += lax.dot_general(
            hot, nominal_ref[:, pl.ds(at, KB)], (((1,), (1,)), ((), ())), preferred_element_type=jnp.float32
        )
        return 0

    lax.fori_loop(0, left_ref.shape[0] // KB, one, 0)
    out_ref[...] = acc[...].astype(jnp.bfloat16)
    yields = background_ref[...] + acc_n[:, 0:1]
    curve_ref[...] = observed_ref[...] / (yields * yields)


def hist_next(bins_ref, rows_ref, out_ref, acc):
    bins_dev = out_ref.shape[0]
    acc[...] = jnp.zeros_like(acc)

    def one(i, _):
        at = pl.multiple_of(i * KB, KB)
        hot = one_hot_of(bins_ref, at, KB, bins_dev)
        acc[...] += jnp.dot(hot, rows_ref[pl.ds(at, KB), :], preferred_element_type=jnp.float32)
        return 0

    lax.fori_loop(0, rows_ref.shape[0] // KB, one, 0)
    out_ref[...] = acc[...].astype(jnp.bfloat16)


def side_of(curve_ref, order, own_ref):
    weighted = (curve_ref[...] * own_ref[...].astype(jnp.float32)).astype(jnp.bfloat16)
    return lax.dot_general(order, weighted, (((1,), (1,)), ((), ())), preferred_element_type=jnp.float32)


def side_first(curve_ref, order_ref, first_ref, out_ref):
    out_ref[...] = side_of(curve_ref, order_ref[:, : 2 * COLS], first_ref).astype(jnp.bfloat16)


def gram_first(slots_ref, curve_ref, order_ref, side_ref, last_ref, *refs):
    firsts, out_ref = refs[:-1], refs[-1]
    lhs = side_ref[...] + side_of(curve_ref, order_ref[:, 2 * COLS :], last_ref).astype(jnp.bfloat16)
    wide, step = firsts[0].shape[1], out_ref.shape[1]
    for k, part in enumerate(firsts):
        full = jnp.dot(lhs, part[...], preferred_element_type=jnp.float32).astype(jnp.bfloat16)
        at = pl.multiple_of(slots_ref[k] * wide, wide)
        for y in range(out_ref.shape[0]):
            out_ref[y, :, pl.ds(at, wide)] = full[y * step : (y + 1) * step]


def gram_last(slots_ref, curve_ref, order_ref, side_ref, *refs):
    lasts, out_ref = refs[:-1], refs[-1]
    lhs = side_ref[...] + side_of(curve_ref, order_ref[:, 2 * COLS :], lasts[0]).astype(jnp.bfloat16)
    wide, step = lasts[0].shape[1], out_ref.shape[1]
    for k, part in enumerate(lasts):
        full = jnp.dot(lhs, part[...], preferred_element_type=jnp.float32).astype(jnp.bfloat16)
        at = pl.multiple_of(slots_ref[k] * wide, wide)
        for y in range(out_ref.shape[0]):
            out_ref[y, :, pl.ds(at, wide)] = full[y * step : (y + 1) * step]


def add_across(turns, first_ref, last_ref, out_ref, wide):
    n0 = out_ref.shape[0]
    lines = first_ref.shape[1] // n0
    first = jnp.sum(first_ref[...].astype(jnp.float32), axis=0)
    last = jnp.sum(last_ref[...].astype(jnp.float32), axis=0)
    wide[...] = jnp.zeros_like(wide)
    for k in range(turns):
        for t in range(3):
            tile, at = (last, k * COLS) if t == 2 else (first, (2 * k + t) * COLS)
            tile = tile[:, at : at + COLS]
            at = (3 * k + t) * lines
            for z in range(n0):
                wide[z, at : at + lines] = tile[z * lines : (z + 1) * lines]
    out_ref[...] = wide[...].astype(jnp.bfloat16)


def add_along(scale, got_ref, out_ref):
    lines = out_ref.shape[0]
    total = jnp.sum(got_ref[...].astype(jnp.float32), axis=0) * scale
    for j in range(out_ref.shape[1] // 128):
        out_ref[:, j * 128 : (j + 1) * 128] = total[j * lines : (j + 1) * lines]


def from_behind(value, axis, steps):
    count = lax.axis_size(axis)
    pairs = [(source, (source + steps) % count) for source in range(count)]
    return lax.ppermute(value, axis, pairs)


def partners(tile):
    count = lax.axis_size("params")
    if count != 8:
        return [from_behind(tile, "params", -k) for k in range(1, count // 2 + 1)], list(range(1, count // 2 + 1))
    pairs = [(source, source ^ 1) for source in range(count)]
    core = lax.rem(lax.axis_index("params"), 2)
    four = from_behind(tile, "params", -4)
    two = from_behind(tile, "params", -2)
    two_other = lax.ppermute(two, "params", pairs)
    other = lax.ppermute(jnp.where(core == 1, tile, four), "params", pairs)
    return [two, four, two_other, other], [2, 4, 3 - 2 * core, 1 + 2 * core]


def exchange(value, axis):
    return lax.all_to_all(value, axis, split_axis=0, concat_axis=0, tiled=True)


def body(event_bins, event_weights, nominal, background, observed):
    bf16, f32 = jnp.bfloat16, jnp.float32
    n0, n1 = (lax.axis_size(a) for a in BINS)
    owners = n0 * n1
    groups = lax.axis_size("params")
    events, width = event_weights.shape
    bins_dev = background.shape[0]
    targets = jnp.arange(owners, dtype=jnp.int32)
    starts = jnp.sum((event_bins[None, :] < targets[:, None] * bins_dev).astype(jnp.int32), axis=1)
    place = lax.axis_index(BINS[1])
    slab = 2 * CAP + EXTRA
    send_a = pl.pallas_call(
        functools.partial(pack_first, owners, bins_dev),
        out_shape=jax.ShapeDtypeStruct((owners, slab, COLS), bf16),
        in_specs=[SMEM, VMEM, VMEM, VMEM],
        out_specs=VMEM,
        compiler_params=PARAMS,
        cost_estimate=cost(4 * owners * CAP * WIN * COLS, 2 * owners * slab * COLS * 2),
        name="pack_first",
    )(starts, event_bins.reshape(-1, 128), nominal.astype(f32).reshape(-1, 128), event_weights)
    got_a = exchange(send_a, BINS)
    sends = pl.pallas_call(
        functools.partial(pack_rest, n0, n1),
        out_shape=[jax.ShapeDtypeStruct((n0, CAP, COLS), bf16)] * n1,
        in_specs=[SMEM, SMEM, VMEM],
        out_specs=[VMEM] * n1,
        compiler_params=PARAMS,
        cost_estimate=cost(2 * owners * CAP * WIN * COLS, 2 * owners * CAP * COLS * 2),
        name="pack_rest",
    )(place.reshape(1).astype(jnp.int32), starts, event_weights)
    mid = jnp.stack([from_behind(x, BINS[1], t) if t else x for t, x in enumerate(sends)], axis=1)
    got_b = exchange(mid, BINS[0])

    total = owners * CAP
    extra = got_a[:, 2 * CAP :, :CAP].astype(f32)
    local = (extra[:, 0] * 32.0 + extra[:, 1]).astype(jnp.int32)
    back = local.reshape(n0, n1, CAP)[:, ::-1]
    local_b = lax.dynamic_slice_in_dim(jnp.concatenate([back, back], axis=1), n1 - 1 - place, n1, axis=1)
    local_b = local_b.reshape(1, total)
    local = local.reshape(1, total)
    nom = jnp.broadcast_to(extra[:, 2].astype(bf16).reshape(1, total), (8, total))
    left, right = (got_a[:, i * CAP : (i + 1) * CAP].reshape(total, COLS) for i in range(2))
    first, curve = pl.pallas_call(
        hist_first,
        out_shape=[jax.ShapeDtypeStruct((bins_dev, 2 * COLS), bf16), jax.ShapeDtypeStruct((bins_dev, 1), f32)],
        in_specs=[VMEM] * 6,
        out_specs=[VMEM] * 2,
        scratch_shapes=[pltpu.VMEM((bins_dev, 2 * COLS), f32), pltpu.VMEM((bins_dev, 8), f32)],
        compiler_params=PARAMS,
        cost_estimate=cost(2 * total * bins_dev * 512, 2 * total * COLS * 2),
        name="hist_first",
    )(local, nom, background.reshape(bins_dev, 1), observed.reshape(bins_dev, 1), left, right)
    lines = width // owners
    j = np.arange(width)
    source = ((j % (width // n1)) // lines * n1 + j // (width // n1)) * lines + j % lines
    order = np.zeros((width, width), np.float32)
    order[j, source] = 1.0
    side = pl.pallas_call(
        side_first,
        out_shape=jax.ShapeDtypeStruct((width, bins_dev), bf16),
        in_specs=[VMEM] * 3,
        out_specs=VMEM,
        compiler_params=PARAMS,
        cost_estimate=cost(2 * bins_dev * width * 2 * COLS, 2 * bins_dev * width * 2),
        name="side_first",
    )(curve, jnp.asarray(order, bf16), first)
    side, got_b = lax.optimization_barrier((side, got_b))
    last = pl.pallas_call(
        hist_next,
        out_shape=jax.ShapeDtypeStruct((bins_dev, COLS), bf16),
        in_specs=[VMEM] * 2,
        out_specs=VMEM,
        scratch_shapes=[pltpu.VMEM((bins_dev, COLS), f32)],
        compiler_params=PARAMS,
        cost_estimate=cost(2 * total * bins_dev * 256, total * COLS * 2),
        name="hist_next",
    )(local_b, got_b.reshape(total, COLS))
    turns = groups // 2 + 1
    firsts, slots = partners(first)
    firsts = [first] + firsts
    lasts = [last] + partners(last)[0]
    slots = jnp.stack([jnp.asarray(k, jnp.int32) for k in [0] + slots])

    part_a = pl.pallas_call(
        gram_first,
        out_shape=jax.ShapeDtypeStruct((n1, width // n1, turns * 2 * COLS), bf16),
        in_specs=[SMEM] + [VMEM] * (4 + turns),
        out_specs=VMEM,
        compiler_params=PARAMS,
        cost_estimate=cost(2 * bins_dev * width * 2 * COLS * (turns + 1), 2 * turns * COLS * bins_dev * 2),
        name="gram_first",
    )(slots, curve, jnp.asarray(order, bf16), side, last, *firsts)
    part_a, side = lax.optimization_barrier((exchange(part_a, BINS[1]), side))
    part_b = pl.pallas_call(
        gram_last,
        out_shape=jax.ShapeDtypeStruct((n1, width // n1, turns * COLS), bf16),
        in_specs=[SMEM] + [VMEM] * (3 + turns),
        out_specs=VMEM,
        compiler_params=PARAMS,
        cost_estimate=cost(2 * bins_dev * width * COLS * turns, turns * COLS * bins_dev * 2),
        name="gram_last",
    )(slots, curve, jnp.asarray(order, bf16), side, *lasts)
    part_b = exchange(part_b, BINS[1])
    packed = -(-lines * turns * width // 128 // 16) * 16
    across = pl.pallas_call(
        functools.partial(add_across, turns),
        out_shape=jax.ShapeDtypeStruct((n0, packed, 128), bf16),
        in_specs=[VMEM] * 2,
        out_specs=VMEM,
        scratch_shapes=[pltpu.VMEM((n0, packed, 128), f32)],
        compiler_params=PARAMS,
        name="add_across",
    )(part_a, part_b)
    return pl.pallas_call(
        functools.partial(add_along, 1.0 / (bins_dev * owners)),
        out_shape=jax.ShapeDtypeStruct((lines, turns * width), f32),
        in_specs=[VMEM],
        out_specs=VMEM,
        compiler_params=PARAMS,
        name="add_along",
    )(exchange(across, BINS[0]))


def solution(mesh):
    split = Mesh(mesh.devices.reshape(16, 4, mesh.shape["params"]), ("bins_0", "bins_1", "params"))
    placed = (P(BINS), P(BINS, "params"), P(BINS), P(BINS), P(BINS))
    return jax.shard_map(
        body, mesh=split, in_specs=placed, out_specs=P(PARAMS_BINS, None), check_vma=False
    )
```
